256 devices in a mesh: dp: 8 (over x, core), mp: 32 (over y, z).
Axes of the slice: x: 4, y: 4, z: 8, core: 2. Of those that a mesh axis runs over, the one named last changes fastest.
Arguments:
- hidden: bfloat16 [3072, 26624], P('dp', 'mp'), may hold values from -6 to 6
- down_weight: bfloat16 [26624, 8192], P('mp', 'dp'), may hold values from -0.0390625 to 0.0390625
- adapter_down: bfloat16 [32, 26624, 64], P('dp', 'mp'), may hold values from -0.0390625 to 0.0390625
- adapter_up: bfloat16 [32, 64, 8192], P('dp', None, 'mp'), may hold values from -0.1875 to 0.1875
- output_grad: bfloat16 [3072, 8192], P('dp', 'mp'), may hold values from -6 to 6
- adapter_per_block: int32 [24], replicated, may hold values from 0 to 31, as said below
- live_rows: int32 [8], replicated, may hold values from 96 to 384, as said below
Outputs:
- layer_out: bfloat16 [3072, 8192], P('dp', 'mp')
- hidden_gradient: bfloat16 [3072, 26624], P('dp', 'mp')
- down_grad: bfloat16 [32, 26624, 64], P('dp', 'mp')
- up_grad: bfloat16 [32, 64, 8192], P('dp', None, 'mp')
The draws below stay inside these ranges and needn't reach their ends.
Inputs may be any that keep to these rules, and one draw needn't show every extreme that they name: `adapter_per_block`: adapter k is owned by index k // 4 of dp; the 3 blocks of one index of dp use adapters of 3 different owners. `live_rows`: some index of dp has all 384 rows live.
All inputs are finite; a program needn't handle non-finite values.
Results may differ from the reference program's by a relative error of at most 0.0055.
Values may be sent and summed in bfloat16 or wider, within the bound.
A program may use at most 128 MiB of HBM per device.

```python
import jax
import jax.numpy as jnp

D = 8192
FF = 26624
R = 64
BLK = 128
BLK_DEV = 3
ADP_DEV = 4
ROWS_DEV = 384
TOKENS = 3072
ADAPTERS = 32
N_DP = 8


def draw_adapter_per_block(key, part):
    key = jax.random.fold_in(key, 11)
    primary_random_key, secondary_random_key, third_key = jax.random.split(key, 3)
    ownership_boost = jax.random.randint(primary_random_key, (N_DP,), 0, 4) * 400
    ranking_scores = jax.random.randint(secondary_random_key, (N_DP, N_DP), 0, 1000) + ownership_boost[None, :]
    row_index = jnp.arange(N_DP, dtype=jnp.int32)[:, None]
    col_index = jnp.arange(N_DP, dtype=jnp.int32)[None, :]
    forced = (row_index == 0) & (col_index == 0) | (row_index == N_DP - 1) & (col_index == N_DP - 1)
    ranking_scores = ranking_scores + jnp.where(forced, 100000, 0).astype(jnp.int32)
    distinct = ranking_scores * N_DP + col_index
    ranked = jnp.argsort(-distinct, axis=1)[:, :BLK_DEV].astype(jnp.int32)
    local_selection = jax.random.randint(third_key, (N_DP, BLK_DEV), 0, ADP_DEV)
    slot_index = jnp.arange(BLK_DEV, dtype=jnp.int32)[None, :]
    local_selection = jnp.where((row_index == 0) & (slot_index == 0), 0, local_selection)
    local_selection = jnp.where((row_index == N_DP - 1) & (slot_index == 0), ADP_DEV - 1, local_selection)
    return (ranked * ADP_DEV + local_selection).reshape(-1).astype(jnp.int32)


def draw_live_rows(key, part):
    key = jax.random.fold_in(key, 23)
    primary_random_key, secondary_random_key = jax.random.split(key)
    counts = jax.random.randint(primary_random_key, (N_DP,), ROWS_DEV // 4, ROWS_DEV + 1)
    chosen = jax.random.randint(secondary_random_key, (), 0, N_DP)
    return jnp.where(jnp.arange(N_DP, dtype=jnp.int32) == chosen, ROWS_DEV, counts).astype(jnp.int32)


def levels(stream_key, extent, cuts, least, high):
    gain, own = 1.0, jax.random.fold_in(stream_key, 6)
    for position, shards_of in cuts:
        steps = jnp.exp(jax.random.uniform(jax.random.fold_in(own, position), (shards_of,), jnp.float32, least / len(cuts), high / len(cuts)))
        gain = gain * jnp.repeat(steps, extent[position] // shards_of).reshape([-1 if axis == position else 1 for axis in range(len(extent))])
    return gain


def scatter_about(own_key, extent, scale, most, shards=(), kind=jnp.bfloat16):
    values = scale * jax.random.normal(own_key, extent, jnp.float32)
    if shards:
        values = values * levels(own_key, extent, shards, -0.22, 0.18)
    return jnp.clip(values, -most, most).astype(kind)


def setup_inputs(seed: int = 0) -> dict:
    key_list = jax.random.split(jax.random.key(seed), 8)
    return {
        "hidden": scatter_about(key_list[0], (TOKENS, FF), 1.0, 6.0, ((0, 8), (1, 32))),
        "down_weight": scatter_about(key_list[1], (FF, D), FF ** -0.5, 0.0390625, ((0, 32), (1, 8))),
        "adapter_down": scatter_about(key_list[2], (ADAPTERS, FF, R), FF ** -0.5, 0.0390625, ((0, 8), (1, 32))),
        "adapter_up": scatter_about(key_list[3], (ADAPTERS, R, D), (16 * R) ** -0.5, 0.1875, ((0, 8), (2, 32))),
        "output_grad": scatter_about(key_list[4], (TOKENS, D), 1.0, 6.0, ((0, 8), (1, 32))),
        "adapter_per_block": draw_adapter_per_block(jax.random.fold_in(key_list[7], 71), 0),
        "live_rows": draw_live_rows(jax.random.fold_in(key_list[7], 71), 0),
    }


def reference(hidden, down_weight, adapter_down, adapter_up, output_grad, adapter_per_block, live_rows):
    token_count = hidden.shape[0]
    row_count = token_count // N_DP
    block_total = adapter_per_block.shape[0]
    positions = jnp.arange(token_count, dtype=jnp.int32)
    limits = jnp.repeat(live_rows, row_count)
    live_mask = ((positions % row_count) < limits)[:, None]
    pick_down = adapter_down[adapter_per_block].astype(jnp.float32)
    pick_up = adapter_up[adapter_per_block].astype(jnp.float32)
    hid_blocks = hidden.reshape(block_total, BLK, FF).astype(jnp.float32)
    down_act = jnp.einsum('btf,bfr->btr', hid_blocks, pick_down).astype(jnp.bfloat16)
    base_out = jnp.dot(hidden, down_weight, preferred_element_type=jnp.float32)
    branch = jnp.einsum('btr,brd->btd', down_act.astype(jnp.float32), pick_up).reshape(token_count, D)
    layer_out = jnp.where(live_mask, base_out + branch, jnp.float32(0.0)).astype(jnp.bfloat16)
    masked_grad = jnp.where(live_mask, output_grad, jnp.zeros_like(output_grad))
    grad_blocks = masked_grad.reshape(block_total, BLK, D).astype(jnp.float32)
    up_act = jnp.einsum('btd,brd->btr', grad_blocks, pick_up).astype(jnp.bfloat16)
    base_back = jnp.dot(masked_grad, down_weight.T, preferred_element_type=jnp.float32)
    side_back = jnp.einsum('btr,bfr->btf', up_act.astype(jnp.float32), pick_down).reshape(token_count, FF)
    hidden_gradient = (base_back + side_back).astype(jnp.bfloat16)
    term_down = jnp.einsum('btf,btr->bfr', hid_blocks, up_act.astype(jnp.float32)).astype(jnp.bfloat16)
    term_up = jnp.einsum('btr,btd->brd', down_act.astype(jnp.float32), grad_blocks).astype(jnp.bfloat16)
    onehot = (adapter_per_block[:, None] == jnp.arange(ADAPTERS, dtype=jnp.int32)[None, :]).astype(jnp.float32)
    down_grad = jnp.einsum('bk,bfr->kfr', onehot, term_down.astype(jnp.float32)).astype(jnp.bfloat16)
    up_grad = jnp.einsum('bk,brd->krd', onehot, term_up.astype(jnp.float32)).astype(jnp.bfloat16)
    return layer_out, hidden_gradient, down_grad, up_grad
```

```python
import jax
import jax.numpy as jnp
from jax import lax
from jax.experimental import pallas as pl
from jax.experimental.pallas import tpu as pltpu
from jax.sharding import PartitionSpec as P

BLK = 128
MESH = pl.DeviceIdType.MESH
f32, bf16 = jnp.float32, jnp.bfloat16


def rem(a, n):
    return lax.rem(a, n)


def kernel(live_ref, hid, w_hbm, grad, branch, side, out, dh,
           Wp, Gg, Zs, Zr, Ys, Yr, Sown, acc, dacc,
           lS, wS, wR, gS, gR, zS, zR, yS, yR):
    dp, mp = lax.axis_index("dp"), lax.axis_index("mp")
    x, c, y, z = dp // 2, rem(dp, 2), mp // 8, rem(mp, 8)

    def dev(dx=0, dc=0, dy=0, dz=0):
        return (rem(x + dx, 4) * 2 + rem(c + dc, 2), rem(y + dy, 4) * 8 + rem(z + dz, 8))

    XP, XM, SIB = dev(dx=1), dev(dx=3), dev(dc=1)
    YP, YM, Y2, ZP, ZM = dev(dy=1), dev(dy=3), dev(dy=2), dev(dz=1), dev(dz=7)

    bar = pltpu.get_barrier_semaphore()
    peers = (XP, XM, SIB, YP, YM, Y2, ZP, ZM)
    for p in peers:
        pl.semaphore_signal(bar, inc=1, device_id=p, device_id_type=MESH)

    wbase = x * 8 + c * 4
    loc = [pltpu.make_async_copy(w_hbm.at[:, pl.ds(256 * i, 256)], Wp.at[wbase + i], lS.at[i]) for i in range(4)]
    for cp in loc:
        cp.start()
    gslot = y * 8 + z
    gl = pltpu.make_async_copy(grad, Gg.at[gslot], lS.at[4])
    gl.start()
    pl.semaphore_wait(bar, len(peers))

    sends = []

    def put(src, dst, ss, rs, to):
        cp = pltpu.make_async_remote_copy(src_ref=src, dst_ref=dst, send_sem=ss, recv_sem=rs, device_id=to, device_id_type=MESH)
        cp.start()
        sends.append(cp)

    def got(dst, ss, rs):
        pltpu.make_async_remote_copy(src_ref=dst, dst_ref=dst, send_sem=ss, recv_sem=rs, device_id=XP, device_id_type=MESH).wait_recv()

    def wsl(dx, i, n, dc=0):
        return Wp.at[pl.ds(rem(x + dx, 4) * 8 + rem(c + dc, 2) * 4 + i, n)]

    def wput(k, dx, i, n, to):
        put(wsl(dx, i, n), wsl(dx, i, n), wS.at[k], wR.at[k], to)

    def wgot(k, dx, i, n, dc=0):
        got(wsl(dx, i, n, dc), wS.at[k], wR.at[k])

    def gsl(dy, j, n):
        return Gg.at[pl.ds(rem(y + dy, 4) * 8 + j, n)]

    def gz(dz, lo=0, n=384):
        return Gg.at[y * 8 + rem(z + dz, 8), pl.ds(lo, n)]

    def gput(k, ref, to):
        put(ref, ref, gS.at[k], gR.at[k], to)

    gl.wait()
    gput(0, gz(0), ZP)
    gput(1, gz(0), ZM)
    for cp in loc:
        cp.wait()
    wput(0, 0, 0, 2, XP)
    wput(2, 0, 2, 2, XM)
    wput(6, 0, 0, 4, SIB)
    wput(1, 0, 2, 2, XP)
    wput(3, 0, 0, 2, XM)

    def product(yt, zt):
        acc[...] = jnp.dot(hid[...], Wp[yt * 8 + zt], preferred_element_type=f32)

    def zcopy(r, slot, h, to):
        s = pltpu.make_async_remote_copy(
            src_ref=Zs.at[r, slot, h], dst_ref=Zr.at[r, slot, h], send_sem=zS.at[r, slot, h],
            recv_sem=zR.at[r, slot, h], device_id=to, device_id_type=MESH)
        return s

    def half(h):
        return acc[pl.ds(192 * h, 192)]

    def level0(r, yt):
        product(yt, rem(z + 4, 8))
        for h, to in ((0, ZM), (1, ZP)):
            Zs[r, 0, h] = half(h).astype(bf16)
            zcopy(r, 0, h, to).start()

    def level1(r, yt):
        for s, to in ((0, ZM), (1, ZP)):
            product(yt, rem(z + (5 if s == 0 else 3), 8))
            slot = 1 + s
            Zs[r, slot, 1 - s] = half(1 - s).astype(bf16)
            zcopy(r, slot, 1 - s, to).start()
            zcopy(r, 0, s, to).wait_recv()
            Zs[r, slot, s] = (half(s) + Zr[r, 0, s].astype(f32)).astype(bf16)
            zcopy(r, slot, s, to).start()

    def level23(r, yt, l):
        for s, to in ((0, ZM), (1, ZP)):
            product(yt, rem(z + (4 + l if s == 0 else 4 - l), 8))
            slot = 2 * l - 1 + s
            for h in (1 - s, s):
                zcopy(r, slot - 2, h, to).wait_recv()
                Zs[r, slot, h] = (half(h) + Zr[r, slot - 2, h].astype(f32)).astype(bf16)
                zcopy(r, slot, h, to).start()

    def ycopy(r, yt):
        j = rem(y - yt + 4, 4)
        return pltpu.make_async_remote_copy(
            src_ref=Ys.at[r], dst_ref=Yr.at[j - 1], send_sem=yS.at[r], recv_sem=yR.at[j - 1],
            device_id=(dp, yt * 8 + z), device_id_type=MESH)

    def level4(r, yt):
        product(yt, z)
        for h in (0, 1):
            for slot in (5, 6):
                zcopy(r, slot, h, ZP).wait_recv()
            acc[pl.ds(192 * h, 192)] = half(h) + (Zr[r, 5, h].astype(f32) + Zr[r, 6, h].astype(f32))

        @pl.when(y == yt)
        def _():
            Sown[...] = acc[...]

        @pl.when(y != yt)
        def _():
            Ys[r] = acc[...].astype(bf16)
            ycopy(r, yt).start()

    def back(m, n=2):
        g = jnp.concatenate([Gg[m + i] for i in range(n)], axis=1)
        w = jnp.concatenate([Wp[m + i] for i in range(n)], axis=1)
        dacc[...] += lax.dot_general(g, w, (((1,), (1,)), ((), ())), preferred_element_type=f32)

    def backs(yt):
        def b(i, _):
            back(yt * 8 + 2 * i)
            return 0
        lax.fori_loop(0, 4, b, 0)

    dacc[...] = side[...]
    y0, y1, y2, y3 = x, rem(x + 3, 4), rem(x + 1, 4), rem(x + 2, 4)

    wgot(6, 0, 0, 4, 1)
    level0(0, y0)
    got(gz(7), gS.at[0], gR.at[0]); gput(2, gz(7), ZP)
    got(gz(1), gS.at[1], gR.at[1]); gput(3, gz(1), ZM)
    level1(0, y0)
    got(gz(6), gS.at[2], gR.at[2]); gput(4, gz(6), ZP)
    got(gz(2), gS.at[3], gR.at[3]); gput(5, gz(2), ZM)
    level23(0, y0, 2)
    got(gz(5), gS.at[4], gR.at[4]); gput(6, gz(5, 0, 192), ZP)
    got(gz(3), gS.at[5], gR.at[5]); gput(7, gz(3, 192, 192), ZM)
    level23(0, y0, 3)
    got(gz(4, 0, 192), gS.at[6], gR.at[6])
    got(gz(4, 192, 192), gS.at[7], gR.at[7])
    gput(8, gsl(0, 0, 4), YP)
    gput(10, gsl(0, 4, 4), YM)
    gput(9, gsl(0, 4, 4), YP)
    gput(11, gsl(0, 0, 4), YM)
    level4(0, y0)

    wgot(0, 3, 0, 2); wput(4, 3, 0, 2, XP); wput(7, 3, 0, 2, SIB)
    wgot(2, 1, 2, 2); wput(5, 1, 2, 2, XM); wput(9, 1, 2, 2, SIB)
    wgot(1, 3, 2, 2); wput(8, 3, 2, 2, SIB)
    wgot(3, 1, 0, 2); wput(10, 1, 0, 2, SIB)
    wgot(7, 3, 0, 2, 1); wgot(8, 3, 2, 2, 1); wgot(9, 1, 2, 2, 1); wgot(10, 1, 0, 2, 1)

    def both(fn, *a):
        def b(i, _):
            fn(1 + i, rem(x + 3 - 2 * i, 4), *a)
            return 0
        lax.fori_loop(0, 2, b, 0)

    both(level0)
    both(level1)
    both(level23, 2)
    got(gsl(3, 0, 4), gS.at[8], gR.at[8]); gput(12, gsl(3, 0, 4), YP)
    got(gsl(1, 4, 4), gS.at[10], gR.at[10]); gput(13, gsl(1, 4, 4), YM)
    both(level23, 3)
    both(level4)

    wgot(4, 2, 0, 2); wput(11, 2, 0, 2, SIB)
    wgot(5, 2, 2, 2); wput(12, 2, 2, 2, SIB)
    wgot(11, 2, 0, 2, 1); wgot(12, 2, 2, 2, 1)
    level0(3, y3)
    got(gsl(3, 4, 4), gS.at[9], gR.at[9])
    got(gsl(1, 0, 4), gS.at[11], gR.at[11])
    got(gsl(2, 0, 4), gS.at[12], gR.at[12])
    got(gsl(2, 4, 4), gS.at[13], gR.at[13])
    level1(3, y3)
    backs(y0)
    level23(3, y3, 2)
    backs(y1)
    level23(3, y3, 3)
    backs(y2)
    level4(3, y3)
    backs(y3)

    live = live_ref[0]
    rows = lax.broadcasted_iota(jnp.int32, (384, 1), 0)
    dh[...] = jnp.where(rows < live, dacc[...], 0.0).astype(bf16)
    for j in range(3):
        pltpu.make_async_remote_copy(src_ref=Yr.at[j], dst_ref=Yr.at[j], send_sem=yS.at[0], recv_sem=yR.at[j], device_id=XP, device_id_type=MESH).wait_recv()
    total = (Sown[...] + branch[...]) + (Yr[0].astype(f32) + Yr[1].astype(f32) + Yr[2].astype(f32))
    out[...] = jnp.where(rows < live, total, 0.0).astype(bf16)

    for cp in sends:
        cp.wait_send()

    def zw(i, _):
        r, slot = i // 7, rem(i, 7)
        for h in (0, 1):
            zcopy(r, slot, h, ZP).wait_send()
        return 0
    lax.fori_loop(0, 28, zw, 0)
    for r, yt in enumerate((y0, y1, y2, y3)):
        @pl.when(y != yt)
        def _():
            ycopy(r, yt).wait_send()


def core_call(live, hid, w, grad, branch, side):
    V = pl.BlockSpec(memory_space=pltpu.VMEM)
    D = pltpu.SemaphoreType.DMA
    return pl.pallas_call(
        kernel,
        out_shape=(jax.ShapeDtypeStruct((384, 256), bf16), jax.ShapeDtypeStruct((384, 832), bf16)),
        in_specs=[pl.BlockSpec(memory_space=pltpu.SMEM), V, pl.BlockSpec(memory_space=pl.ANY), V, V, V],
        out_specs=(V, V),
        scratch_shapes=[
            pltpu.VMEM((32, 832, 256), bf16),
            pltpu.VMEM((32, 384, 256), bf16),
            pltpu.VMEM((4, 7, 2, 192, 256), bf16),
            pltpu.VMEM((4, 7, 2, 192, 256), bf16),
            pltpu.VMEM((4, 384, 256), bf16),
            pltpu.VMEM((3, 384, 256), bf16),
            pltpu.VMEM((384, 256), f32),
            pltpu.VMEM((384, 256), f32),
            pltpu.VMEM((384, 832), f32),
            D((5,)), D((13,)), D((13,)), D((14,)), D((14,)),
            D((4, 7, 2)), D((4, 7, 2)), D((4,)), D((3,)),
        ],
        name="base_layer",
        cost_estimate=pl.CostEstimate(flops=2 * 2 * 384 * 832 * 8192, bytes_accessed=6 * 2 ** 20, transcendentals=0),
        compiler_params=pltpu.CompilerParams(collective_id=0, has_side_effects=True, vmem_limit_bytes=58 * 2 ** 20),
    )(live, hid, w, grad, branch, side)


def shards(hidden, down_weight, adapter_down, adapter_up, output_grad, adapter_per_block, live_rows):
    dp_count = lax.axis_size("dp")
    dp_index = lax.axis_index("dp")
    row_count = hidden.shape[0]
    local_unit_index = hidden.shape[1]
    model_local = output_grad.shape[1]
    owned_count = adapter_down.shape[0]
    block_count = row_count // BLK
    id_table = adapter_per_block.reshape(dp_count, block_count)
    own_ids = lax.dynamic_slice_in_dim(id_table, dp_index, 1, 0)[0]
    own_owners = own_ids // owned_count
    live_count = lax.dynamic_slice_in_dim(live_rows, dp_index, 1, 0)
    live_mask = (jnp.arange(row_count, dtype=jnp.int32) < live_count[0])[:, None]
    masked_grad = jnp.where(live_mask, output_grad, jnp.zeros_like(output_grad))
    source_ids = jnp.arange(dp_count, dtype=jnp.int32)
    local_ids = dp_index * owned_count + jnp.arange(owned_count, dtype=jnp.int32)
    wanted = jnp.sum((id_table[:, :, None] == local_ids[None, None, :]).astype(jnp.int32), axis=1).astype(jnp.bfloat16)
    every_down, every_up = (lax.all_gather(adapter_down, "dp", axis=0, tiled=True), lax.all_gather(adapter_up, "dp", axis=0, tiled=True))
    all_ids = jnp.arange(owned_count * dp_count, dtype=jnp.int32)
    select = (own_ids[:, None] == all_ids[None, :]).astype(jnp.bfloat16)
    block_down = jnp.einsum("bk,kfr->bfr", select, every_down, preferred_element_type=jnp.float32).astype(jnp.bfloat16)
    block_up = jnp.einsum("bk,krd->brd", select, every_up, preferred_element_type=jnp.float32).astype(jnp.bfloat16)
    hid_blocks = hidden.reshape(block_count, BLK, local_unit_index)
    grad_blocks = masked_grad.reshape(block_count, BLK, model_local)
    down_part = jnp.einsum("btf,bfr->btr", hid_blocks, block_down, preferred_element_type=jnp.float32)
    up_part = jnp.einsum("btd,brd->btr", grad_blocks, block_up, preferred_element_type=jnp.float32)
    down_sum, up_sum = lax.psum((down_part, up_part), "mp")
    down_act = down_sum.astype(jnp.bfloat16)
    up_act = up_sum.astype(jnp.bfloat16)
    branch = jnp.einsum("btr,brd->btd", down_act, block_up, preferred_element_type=jnp.float32).reshape(row_count, model_local)
    side_back = jnp.einsum("btr,bfr->btf", up_act, block_down, preferred_element_type=jnp.float32).reshape(row_count, local_unit_index)
    layer_out, hidden_gradient = core_call(live_count, hidden, down_weight, output_grad, branch, side_back)
    term_down = jnp.einsum("btf,btr->bfr", hid_blocks, up_act, preferred_element_type=jnp.float32).astype(jnp.bfloat16)
    term_up = jnp.einsum("btr,btd->brd", down_act, grad_blocks, preferred_element_type=jnp.float32).astype(jnp.bfloat16)
    routing = (source_ids[:, None] == own_owners[None, :]).astype(jnp.bfloat16)
    back_down = jnp.einsum("ob,bfr->ofr", routing, term_down, preferred_element_type=jnp.float32).astype(jnp.bfloat16)
    back_up = jnp.einsum("ob,brd->ord", routing, term_up, preferred_element_type=jnp.float32).astype(jnp.bfloat16)
    arrived_down, arrived_up = (
        lax.all_to_all(back_down, "dp", split_axis=0, concat_axis=0, tiled=True),
        lax.all_to_all(back_up, "dp", split_axis=0, concat_axis=0, tiled=True),
    )
    down_grad = jnp.einsum("sa,sfr->afr", wanted, arrived_down, preferred_element_type=jnp.float32).astype(jnp.bfloat16)
    up_grad = jnp.einsum("sa,srd->ard", wanted, arrived_up, preferred_element_type=jnp.float32).astype(jnp.bfloat16)
    return (layer_out, hidden_gradient, down_grad, up_grad)


def solution(mesh):
    return jax.shard_map(
        shards,
        mesh=mesh,
        in_specs=(P("dp", "mp"), P("mp", "dp"), P("dp", "mp", None), P("dp", None, "mp"), P("dp", "mp"), P(), P()),
        out_specs=(P("dp", "mp"), P("dp", "mp"), P("dp", "mp", None), P("dp", None, "mp")),
        check_vma=False,
    )
```

```python
import jax
import jax.numpy as jnp
from jax import lax
from jax.experimental import pallas as pl
from jax.experimental.pallas import tpu as pltpu
from jax.sharding import PartitionSpec as P

BLK = 128
MESH = pl.DeviceIdType.MESH
f32, bf16 = jnp.float32, jnp.bfloat16


def rem(a, n):
    return lax.rem(a, n)


def kernel(ids, lives, hid_t, w_hbm, a_ref, b_ref, grad, out, dh, dg, ug,
           hid, masked, Wp, Gg, Zs, Zr, Ys, Yr, Sown, acc, dacc,
           As, Ar, Bs, Br, Ts, Tr, Us, Ur, terms, uterms, part, part_r, fold, fold_r, act,
           lS, wS, wR, gS, gR, zS, zR, yS, yR, aS, aR, bS, bR, tS, tR, uS, uR, p1S, p1R, p2S, p2R, p3S, p3R):
    dp, mp = lax.axis_index("dp"), lax.axis_index("mp")
    x, c, y, z = dp // 2, rem(dp, 2), mp // 8, rem(mp, 8)

    def dev(dx=0, dc=0, dy=0, dz=0):
        return (rem(x + dx, 4) * 2 + rem(c + dc, 2), rem(y + dy, 4) * 8 + rem(z + dz, 8))

    XP, XM, SIB = dev(dx=1), dev(dx=3), dev(dc=1)
    YP, YM, Y2, ZP, ZM = dev(dy=1), dev(dy=3), dev(dy=2), dev(dz=1), dev(dz=7)

    bar = pltpu.get_barrier_semaphore()
    dps = [(rem(dp + k, 8), mp) for k in range(8)]
    ys = [dev(dy=k) for k in range(4)]
    zs = [dev(dz=k) for k in range(8)]
    peers = dps[1:] + ys[1:] + zs[1:]
    for p in peers:
        pl.semaphore_signal(bar, inc=1, device_id=p, device_id_type=MESH)

    wbase = x * 8 + c * 4
    loc = [pltpu.make_async_copy(w_hbm.at[:, pl.ds(256 * i, 256)], Wp.at[wbase + i], lS.at[i]) for i in range(4)]
    for cp in loc:
        cp.start()
    gslot = y * 8 + z
    gl = pltpu.make_async_copy(grad, Gg.at[gslot], lS.at[4])
    gl.start()

    def wanted(d):
        found, sel = jnp.int32(0), jnp.int32(0)
        for b in range(3):
            i = ids[3 * d + b]
            hit = (i // 4) == dp
            found = jnp.where(hit, 1, found)
            sel = jnp.where(hit, i % 4, sel)
        return found, sel

    own = [ids[3 * dp + b] // 4 for b in range(3)]

    def block_for(o):
        sel = jnp.int32(0)
        for b in range(1, 3):
            sel = jnp.where(own[b] == o, b, sel)
        return sel

    live = lives[dp]
    rows = lax.broadcasted_iota(jnp.int32, (384, 1), 0)
    for k in range(8):
        _, sel = wanted(dps[k][0])
        (Ar if k == 0 else As)[k] = a_ref[sel]
        (Br if k == 0 else Bs)[k] = b_ref[sel]
    hid[...] = hid_t[...].T
    masked[...] = jnp.where(rows < live, grad[...], jnp.zeros_like(grad))
    pl.semaphore_wait(bar, len(peers))

    sends = []

    def put(src, dst, ss, rs, to):
        cp = pltpu.make_async_remote_copy(src_ref=src, dst_ref=dst, send_sem=ss, recv_sem=rs, device_id=to, device_id_type=MESH)
        cp.start()
        sends.append(cp)

    def got(dst, ss, rs):
        pltpu.make_async_remote_copy(src_ref=dst, dst_ref=dst, send_sem=ss, recv_sem=rs, device_id=XP, device_id_type=MESH).wait_recv()

    def wsl(dx, i, n, dc=0):
        return Wp.at[pl.ds(rem(x + dx, 4) * 8 + rem(c + dc, 2) * 4 + i, n)]

    def wput(k, dx, i, n, to):
        put(wsl(dx, i, n), wsl(dx, i, n), wS.at[k], wR.at[k], to)

    def wgot(k, dx, i, n, dc=0):
        got(wsl(dx, i, n, dc), wS.at[k], wR.at[k])

    def gsl(dy, j, n):
        return Gg.at[pl.ds(rem(y + dy, 4) * 8 + j, n)]

    def gz(dz, lo=0, n=384):
        return Gg.at[y * 8 + rem(z + dz, 8), pl.ds(lo, n)]

    def gput(k, ref, to):
        put(ref, ref, gS.at[k], gR.at[k], to)

    for k in range(1, 8):
        put(Bs.at[k], Br.at[k], bS.at[k], bR.at[k], dps[k])
    for k in range(1, 8):
        put(As.at[k], Ar.at[k], aS.at[k], aR.at[k], dps[k])
    gl.wait()
    gput(0, gz(0), ZP)
    gput(1, gz(0), ZM)
    for cp in loc:
        cp.wait()
    wput(0, 0, 0, 2, XP)
    wput(2, 0, 2, 2, XM)
    wput(6, 0, 0, 4, SIB)
    wput(1, 0, 2, 2, XP)
    wput(3, 0, 0, 2, XM)

    def product(yt, zt):
        acc[...] = jnp.dot(hid[...], Wp[yt * 8 + zt], preferred_element_type=f32)

    def zcopy(r, slot, h, to):
        s = pltpu.make_async_remote_copy(
            src_ref=Zs.at[r, slot, h], dst_ref=Zr.at[r, slot, h], send_sem=zS.at[r, slot, h],
            recv_sem=zR.at[r, slot, h], device_id=to, device_id_type=MESH)
        return s

    def half(h):
        return acc[pl.ds(192 * h, 192)]

    def level0(r, yt):
        product(yt, rem(z + 4, 8))
        for h, to in ((0, ZM), (1, ZP)):
            Zs[r, 0, h] = half(h).astype(bf16)
            zcopy(r, 0, h, to).start()

    def level1(r, yt):
        for s, to in ((0, ZM), (1, ZP)):
            product(yt, rem(z + (5 if s == 0 else 3), 8))
            slot = 1 + s
            Zs[r, slot, 1 - s] = half(1 - s).astype(bf16)
            zcopy(r, slot, 1 - s, to).start()
            zcopy(r, 0, s, to).wait_recv()
            Zs[r, slot, s] = (half(s) + Zr[r, 0, s].astype(f32)).astype(bf16)
            zcopy(r, slot, s, to).start()

    def level23(r, yt, l):
        for s, to in ((0, ZM), (1, ZP)):
            product(yt, rem(z + (4 + l if s == 0 else 4 - l), 8))
            slot = 2 * l - 1 + s
            for h in (1 - s, s):
                zcopy(r, slot - 2, h, to).wait_recv()
                Zs[r, slot, h] = (half(h) + Zr[r, slot - 2, h].astype(f32)).astype(bf16)
                zcopy(r, slot, h, to).start()

    def ycopy(r, yt):
        j = rem(y - yt + 4, 4)
        return pltpu.make_async_remote_copy(
            src_ref=Ys.at[r], dst_ref=Yr.at[j - 1], send_sem=yS.at[r], recv_sem=yR.at[j - 1],
            device_id=(dp, yt * 8 + z), device_id_type=MESH)

    def level4(r, yt):
        product(yt, z)
        for h in (0, 1):
            for slot in (5, 6):
                zcopy(r, slot, h, ZP).wait_recv()
            acc[pl.ds(192 * h, 192)] = half(h) + (Zr[r, 5, h].astype(f32) + Zr[r, 6, h].astype(f32))

        @pl.when(y == yt)
        def _():
            Sown[...] = acc[...]

        @pl.when(y != yt)
        def _():
            Ys[r] = acc[...].astype(bf16)
            ycopy(r, yt).start()

    def back(m, n=2):
        g = jnp.concatenate([Gg[m + i] for i in range(n)], axis=1)
        w = jnp.concatenate([Wp[m + i] for i in range(n)], axis=1)
        dacc[...] += lax.dot_general(w, g, (((1,), (1,)), ((), ())), preferred_element_type=f32)

    def backs(yt):
        def b(i, _):
            back(yt * 8 + 2 * i)
            return 0
        lax.fori_loop(0, 4, b, 0)

    TB = (((1,), (1,)), ((), ()))
    TA = (((0,), (0,)), ((), ()))
    slot = [rem(dp - own[b] + 8, 8) for b in range(3)]

    def dslice(k, n=48):
        return pl.ds(pl.multiple_of(k * 48, 16), n)

    def rank_parts():
        for k in range(1, 8):
            got(Br.at[k], bS.at[k], bR.at[k])
        for k in range(1, 8):
            got(Ar.at[k], aS.at[k], aR.at[k])
        for b in range(3):
            r = pl.ds(128 * b, 128)
            dn = lax.dot_general(hid[r], Ar[slot[b]], TB, preferred_element_type=f32)
            up = lax.dot_general(masked[r], Br[slot[b]], TB, preferred_element_type=f32)
            part[r] = jnp.concatenate([dn, up], axis=1)
        for k in range(1, 8):
            put(part.at[dslice(rem(z + k, 8))], part_r.at[k], p1S.at[k], p1R.at[k], zs[k])

    def rank_fold_z():
        v = part[dslice(z)]
        for k in range(1, 8):
            got(part_r.at[k], p1S.at[k], p1R.at[k])
            v = v + part_r[k]
        fold[...] = v
        for k in range(1, 4):
            put(fold, fold_r.at[k], p2S.at[k], p2R.at[k], ys[k])

    def rank_fold_y():
        v = fold[...]
        for k in range(1, 4):
            got(fold_r.at[k], p2S.at[k], p2R.at[k])
            v = v + fold_r[k]
        act[dslice(z)] = v.astype(bf16)
        mine = act.at[dslice(z)]
        for k in range(1, 8):
            put(mine, mine, p3S.at[k], p3R.at[k], zs[k])

    def rank_terms():
        for k in range(1, 8):
            theirs = act.at[dslice(rem(z + 8 - k, 8))]
            got(theirs, p3S.at[k], p3R.at[k])
        for b in range(3):
            r = pl.ds(128 * b, 128)
            u = act[r]
            dn, up = u[:, :64], u[:, 64:]
            terms[b] = lax.dot_general(up, hid[r], TA, preferred_element_type=f32).astype(bf16)
            uterms[b] = lax.dot_general(dn, masked[r], TA, preferred_element_type=f32).astype(bf16)
        for k in range(8):
            sel = block_for(dps[k][0])
            (Tr if k == 0 else Ts)[k] = terms[sel]
            (Ur if k == 0 else Us)[k] = uterms[sel]
        for k in range(1, 8):
            put(Ts.at[k], Tr.at[k], tS.at[k], tR.at[k], dps[k])
            put(Us.at[k], Ur.at[k], uS.at[k], uR.at[k], dps[k])

    def rank_side():
        for b in range(3):
            up = act[pl.ds(128 * b, 128)][:, 64:]
            a_t = Ar[slot[b]].T
            dacc[:, pl.ds(128 * b, 128)] = lax.dot_general(a_t, up, TB, preferred_element_type=f32)

    def rank_out():
        for k in range(1, 8):
            got(Tr.at[k], tS.at[k], tR.at[k])
            got(Ur.at[k], uS.at[k], uR.at[k])
        picks = [wanted(rem(dp - k + 8, 8)) for k in range(8)]
        for a in range(4):
            w = [jnp.where((f == 1) & (s == a), 1.0, 0.0).astype(f32) for f, s in picks]
            v = w[0] * Tr[0].astype(f32)
            u = w[0] * Ur[0].astype(f32)
            for k in range(1, 8):
                v = v + w[k] * Tr[k].astype(f32)
                u = u + w[k] * Ur[k].astype(f32)
            dg[a] = v.astype(bf16)
            ug[a] = u.astype(bf16)

    y0, y1, y2, y3 = x, rem(x + 3, 4), rem(x + 1, 4), rem(x + 2, 4)

    wgot(6, 0, 0, 4, 1)
    level0(0, y0)
    got(gz(7), gS.at[0], gR.at[0]); gput(2, gz(7), ZP)
    got(gz(1), gS.at[1], gR.at[1]); gput(3, gz(1), ZM)
    level1(0, y0)
    rank_parts()
    got(gz(6), gS.at[2], gR.at[2]); gput(4, gz(6), ZP)
    got(gz(2), gS.at[3], gR.at[3]); gput(5, gz(2), ZM)
    level23(0, y0, 2)
    got(gz(5), gS.at[4], gR.at[4]); gput(6, gz(5, 0, 192), ZP)
    got(gz(3), gS.at[5], gR.at[5]); gput(7, gz(3, 192, 192), ZM)
    level23(0, y0, 3)
    got(gz(4, 0, 192), gS.at[6], gR.at[6])
    got(gz(4, 192, 192), gS.at[7], gR.at[7])
    gput(8, gsl(0, 0, 4), YP)
    gput(10, gsl(0, 4, 4), YM)
    gput(9, gsl(0, 4, 4), YP)
    gput(11, gsl(0, 0, 4), YM)
    level4(0, y0)
    rank_fold_z()

    wgot(0, 3, 0, 2); wput(4, 3, 0, 2, XP); wput(7, 3, 0, 2, SIB)
    wgot(2, 1, 2, 2); wput(5, 1, 2, 2, XM); wput(9, 1, 2, 2, SIB)
    wgot(1, 3, 2, 2); wput(8, 3, 2, 2, SIB)
    wgot(3, 1, 0, 2); wput(10, 1, 0, 2, SIB)
    wgot(7, 3, 0, 2, 1); wgot(8, 3, 2, 2, 1); wgot(9, 1, 2, 2, 1); wgot(10, 1, 0, 2, 1)

    rank_fold_y()

    def both(fn, *a):
        def b(i, _):
            fn(1 + i, rem(x + 3 - 2 * i, 4), *a)
            return 0
        lax.fori_loop(0, 2, b, 0)

    both(level0)
    both(level1)
    rank_terms()
    rank_side()
    both(level23, 2)
    got(gsl(3, 0, 4), gS.at[8], gR.at[8]); gput(12, gsl(3, 0, 4), YP)
    got(gsl(1, 4, 4), gS.at[10], gR.at[10]); gput(13, gsl(1, 4, 4), YM)
    both(level23, 3)
    both(level4)

    wgot(4, 2, 0, 2); wput(11, 2, 0, 2, SIB)
    wgot(5, 2, 2, 2); wput(12, 2, 2, 2, SIB)
    wgot(11, 2, 0, 2, 1); wgot(12, 2, 2, 2, 1)
    level0(3, y3)
    got(gsl(3, 4, 4), gS.at[9], gR.at[9])
    got(gsl(1, 0, 4), gS.at[11], gR.at[11])
    got(gsl(2, 0, 4), gS.at[12], gR.at[12])
    got(gsl(2, 4, 4), gS.at[13], gR.at[13])
    level1(3, y3)
    backs(y0)
    level23(3, y3, 2)
    backs(y1)
    level23(3, y3, 3)
    backs(y2)
    level4(3, y3)
    backs(y3)

    columns = lax.broadcasted_iota(jnp.int32, (1, 384), 1)
    dh[...] = jnp.where(columns < live, dacc[...], 0.0).astype(bf16)
    rank_out()
    for j in range(3):
        pltpu.make_async_remote_copy(src_ref=Yr.at[j], dst_ref=Yr.at[j], send_sem=yS.at[0], recv_sem=yR.at[j], device_id=XP, device_id_type=MESH).wait_recv()
    total = Sown[...] + (Yr[0].astype(f32) + Yr[1].astype(f32) + Yr[2].astype(f32))
    for b in range(3):
        r = pl.ds(128 * b, 128)
        branch = jnp.dot(act[r][:, :64], Br[slot[b]], preferred_element_type=f32)
        t = total[128 * b:128 * b + 128] + branch
        out[r] = jnp.where(rows[128 * b:128 * b + 128] < live, t, 0.0).astype(bf16)

    for cp in sends:
        cp.wait_send()

    def zw(i, _):
        r, slot = i // 7, rem(i, 7)
        for h in (0, 1):
            zcopy(r, slot, h, ZP).wait_send()
        return 0
    lax.fori_loop(0, 28, zw, 0)
    for r, yt in enumerate((y0, y1, y2, y3)):
        @pl.when(y != yt)
        def _():
            ycopy(r, yt).wait_send()


def shards(hidden, down_weight, adapter_down, adapter_up, output_grad, adapter_per_block, live_rows):
    V = pl.BlockSpec(memory_space=pltpu.VMEM)
    S = pl.BlockSpec(memory_space=pltpu.SMEM)
    D = pltpu.SemaphoreType.DMA
    M = pltpu.VMEM
    out, dh_t, dg_t, ug = pl.pallas_call(
        kernel,
        out_shape=(
            jax.ShapeDtypeStruct((384, 256), bf16), jax.ShapeDtypeStruct((832, 384), bf16),
            jax.ShapeDtypeStruct((4, 64, 832), bf16), jax.ShapeDtypeStruct((4, 64, 256), bf16)),
        in_specs=[S, S, V, pl.BlockSpec(memory_space=pl.ANY), V, V, V],
        out_specs=(V, V, V, V),
        scratch_shapes=[
            M((384, 832), bf16),
            M((384, 256), bf16),
            M((32, 832, 256), bf16),
            M((32, 384, 256), bf16),
            M((4, 7, 2, 192, 256), bf16),
            M((4, 7, 2, 192, 256), bf16),
            M((4, 384, 256), bf16),
            M((3, 384, 256), bf16),
            M((384, 256), f32),
            M((384, 256), f32),
            M((832, 384), f32),
            M((8, 64, 832), bf16), M((8, 64, 832), bf16), M((8, 64, 256), bf16), M((8, 64, 256), bf16),
            M((8, 64, 832), bf16), M((8, 64, 832), bf16), M((8, 64, 256), bf16), M((8, 64, 256), bf16),
            M((3, 64, 832), bf16), M((3, 64, 256), bf16),
            M((384, 128), f32), M((8, 48, 128), f32), M((48, 128), f32), M((4, 48, 128), f32), M((384, 128), bf16),
            D((5,)), D((13,)), D((13,)), D((14,)), D((14,)),
            D((4, 7, 2)), D((4, 7, 2)), D((4,)), D((3,)),
            D((8,)), D((8,)), D((8,)), D((8,)), D((8,)), D((8,)), D((8,)), D((8,)),
            D((8,)), D((8,)), D((4,)), D((4,)), D((8,)), D((8,)),
        ],
        name="layer",
        cost_estimate=pl.CostEstimate(flops=2 * 2 * 384 * 832 * 8192, bytes_accessed=6 * 2 ** 20, transcendentals=0),
        compiler_params=pltpu.CompilerParams(collective_id=0, has_side_effects=True, vmem_limit_bytes=58 * 2 ** 20),
    )(adapter_per_block, live_rows, hidden.T, down_weight, jnp.swapaxes(adapter_down, 1, 2), adapter_up, output_grad)
    return out, dh_t.T, jnp.swapaxes(dg_t, 1, 2), ug


def solution(mesh):
    return jax.shard_map(
        shards,
        mesh=mesh,
        in_specs=(P("dp", "mp"), P("mp", "dp"), P("dp", "mp", None), P("dp", None, "mp"), P("dp", "mp"), P(), P()),
        out_specs=(P("dp", "mp"), P("dp", "mp"), P("dp", "mp", None), P("dp", None, "mp")),
        check_vma=False,
    )
```

```python
import jax
import jax.numpy as jnp
from jax import lax
from jax.experimental import pallas as pl
from jax.experimental.pallas import tpu as pltpu
from jax.sharding import PartitionSpec as P

BLK = 128
MESH = pl.DeviceIdType.MESH
f32, bf16 = jnp.float32, jnp.bfloat16
TB = (((1,), (1,)), ((), ()))
TA = (((0,), (0,)), ((), ()))


def rem(a, n):
    return lax.rem(a, n)


def kernel(ids, lives, hid_h, w_hbm, a_h, b_h, grad_h, out, dh, dg, ug,
           hid_t, hid, grad, masked, a_ref, b_ref, Wp, Gg, Zs, Zr, Ys, Yr, Sown, acc, dacc,
           As, Ar, Bs, Br, Ts, Tr, Us, Ur, terms, uterms, part, part_r, fold, fold_r, act, down_act, up_act,
           lS, wS, wR, w1S, w1R, gS, gR, gyS, gyR, gfS, gfR, zS, zR, yS, yR,
           aS, aR, bS, bR, tS, tR, uS, uR, p1S, p1R, p2S, p2R, p3S, p3R):
    dp, mp = lax.axis_index("dp"), lax.axis_index("mp")
    x, c, y, z = dp // 2, rem(dp, 2), mp // 8, rem(mp, 8)

    def dev(dx=0, dc=0, dy=0, dz=0):
        return (rem(x + dx, 4) * 2 + rem(c + dc, 2), rem(y + dy, 4) * 8 + rem(z + dz, 8))

    XP, XM, SIB = dev(dx=1), dev(dx=3), dev(dc=1)
    dps = [(rem(dp + k, 8), mp) for k in range(8)]
    ys = [dev(dy=k) for k in range(4)]
    zs = [dev(dz=k) for k in range(8)]
    YP, YM, ZP, ZM = ys[1], ys[3], zs[1], zs[7]

    bar = pltpu.get_barrier_semaphore()
    peers = dps[1:] + ys[1:] + zs[1:]
    for p in peers:
        pl.semaphore_signal(bar, inc=1, device_id=p, device_id_type=MESH)

    wbase = x * 8 + c * 4
    loc = [pltpu.make_async_copy(s, d, lS.at[i]) for i, (s, d) in enumerate(
        [(b_h, b_ref), (grad_h, grad), (grad_h, Gg.at[y * 8 + z]), (a_h, a_ref), (hid_h, hid_t)]
        + [(w_hbm.at[:, pl.ds(256 * i, 256)], Wp.at[wbase + i]) for i in range(4)])]
    for cp in loc:
        cp.start()

    def wanted(d):
        found, sel = jnp.int32(0), jnp.int32(0)
        for b in range(3):
            i = ids[3 * d + b]
            hit = (i // 4) == dp
            found = jnp.where(hit, 1, found)
            sel = jnp.where(hit, i % 4, sel)
        return found, sel

    own = [ids[3 * dp + b] // 4 for b in range(3)]

    def block_for(o):
        sel = jnp.int32(0)
        for b in range(1, 3):
            sel = jnp.where(own[b] == o, b, sel)
        return sel

    live = lives[dp]
    rows = lax.broadcasted_iota(jnp.int32, (384, 1), 0)
    slot = [rem(dp - own[b] + 8, 8) for b in range(3)]
    sels = [wanted(dps[k][0])[1] for k in range(8)]

    sends = []

    def put(src, dst, ss, rs, to):
        cp = pltpu.make_async_remote_copy(src_ref=src, dst_ref=dst, send_sem=ss, recv_sem=rs, device_id=to, device_id_type=MESH)
        cp.start()
        sends.append(cp)

    def got(dst, ss, rs):
        pltpu.make_async_remote_copy(src_ref=dst, dst_ref=dst, send_sem=ss, recv_sem=rs, device_id=XP, device_id_type=MESH).wait_recv()

    def wsl(dx, i, n, dc=0):
        return Wp.at[pl.ds(rem(x + dx, 4) * 8 + rem(c + dc, 2) * 4 + i, n)]

    def wput(k, dx, i, n, to):
        put(wsl(dx, i, n), wsl(dx, i, n), wS.at[k], wR.at[k], to)

    def wgot(k, dx, i, n, dc=0):
        got(wsl(dx, i, n, dc), wS.at[k], wR.at[k])

    ORDER = (0, 7, 1, 6, 2, 5, 3, 4)

    def gsl(dy, dz, lo=0, n=384):
        return Gg.at[rem(y + dy, 4) * 8 + rem(z + dz, 8), pl.ds(lo, n)]

    def gput(k, ref, to):
        put(ref, ref, gS.at[k], gR.at[k], to)

    def gz(k):
        if k < 4:
            lo, hi = gsl(0, 8 - k), gsl(0, k)
            got(lo, gS.at[2 * k - 2], gR.at[2 * k - 2])
            got(hi, gS.at[2 * k - 1], gR.at[2 * k - 1])
            if k == 3:
                lo, hi = gsl(0, 5, 0, 192), gsl(0, 3, 192, 192)
            gput(2 * k, lo, ZP)
            gput(2 * k + 1, hi, ZM)
        else:
            got(gsl(0, 4, 0, 192), gS.at[6], gR.at[6])
            got(gsl(0, 4, 192, 192), gS.at[7], gR.at[7])

    def gy(j):
        ref = gsl(0, ORDER[j])
        put(ref, ref, gyS.at[j, 0], gyR.at[j, 0], YP)
        put(ref, ref, gyS.at[j, 1], gyR.at[j, 1], YM)

    def gf(j):
        got(gsl(3, ORDER[j]), gyS.at[j, 0], gyR.at[j, 0])
        ref = gsl(3, ORDER[j], 0, 192)
        put(ref, ref, gfS.at[j, 0], gfR.at[j, 0], YP)
        got(gsl(1, ORDER[j]), gyS.at[j, 1], gyR.at[j, 1])
        ref = gsl(1, ORDER[j], 192, 192)
        put(ref, ref, gfS.at[j, 1], gfR.at[j, 1], YM)

    def gl(j):
        got(gsl(2, ORDER[j], 0, 192), gfS.at[j, 0], gfR.at[j, 0])
        got(gsl(2, ORDER[j], 192, 192), gfS.at[j, 1], gfR.at[j, 1])

    def row(r, zt):
        if r in (0, 3):
            return rem(x + (0 if r == 0 else 2), 4)
        left = rem(zt, 4) < 2
        return rem(x + jnp.where(left, 3, 1) if r == 1 else x + jnp.where(left, 1, 3), 4)

    def pre(r, level):
        b = r // 3
        if level in (0, 4):
            zt = rem(z + 4, 8) if level == 0 else z
            acc[b, 0] = jnp.dot(hid[...], Wp[row(r, zt) * 8 + zt], preferred_element_type=f32)
            return
        for s in (0, 1):
            zt = rem(z + (4 + level if s == 0 else 4 - level), 8)
            acc[b, s] = jnp.dot(hid[...], Wp[row(r, zt) * 8 + zt], preferred_element_type=f32)

    def zcopy(r, k, h, to):
        return pltpu.make_async_remote_copy(
            src_ref=Zs.at[r, k, h], dst_ref=Zr.at[r, k, h], send_sem=zS.at[r, k, h],
            recv_sem=zR.at[r, k, h], device_id=to, device_id_type=MESH)

    def half(r, s, h):
        return acc[r // 3, s, pl.ds(192 * h, 192)]

    def send(r, k, h, to, v):
        Zs[r, k, h] = v.astype(bf16)
        zcopy(r, k, h, to).start()

    def level0(r):
        for h, to in ((0, ZM), (1, ZP)):
            send(r, 0, h, to, half(r, 0, h))

    def level1(r):
        for s, to in ((0, ZM), (1, ZP)):
            send(r, 1 + s, 1 - s, to, half(r, s, 1 - s))
        for s, to in ((0, ZM), (1, ZP)):
            zcopy(r, 0, s, to).wait_recv()
            send(r, 1 + s, s, to, half(r, s, s) + Zr[r, 0, s].astype(f32))

    def level23(r, l):
        for i in (0, 1):
            for s, to in ((0, ZM), (1, ZP)):
                k, h = 2 * l - 1 + s, (1 - s if i == 0 else s)
                zcopy(r, k - 2, h, to).wait_recv()
                send(r, k, h, to, half(r, s, h) + Zr[r, k - 2, h].astype(f32))

    def level(r, l):
        if l == 0:
            level0(r)
        elif l == 1:
            level1(r)
        elif l < 4:
            level23(r, l)
        else:
            level4(r)

    def both(r, l):
        pre(r, l)
        level(r, l)

    def ycopy(r, h):
        yt = row(r, z)
        j = rem(y - yt + 4, 4)
        return pltpu.make_async_remote_copy(
            src_ref=Ys.at[r, h], dst_ref=Yr.at[j - 1, h], send_sem=yS.at[r, h], recv_sem=yR.at[j - 1, h],
            device_id=(dp, yt * 8 + z), device_id_type=MESH)

    def level4(r):
        for h in (0, 1):
            for k in (5, 6):
                zcopy(r, k, h, ZP).wait_recv()
            v = half(r, 0, h) + (Zr[r, 5, h].astype(f32) + Zr[r, 6, h].astype(f32))
            Ys[r, h] = v.astype(bf16)

            @pl.when(y == row(r, z))
            def _():
                Sown[pl.ds(192 * h, 192)] = v

            @pl.when(y != row(r, z))
            def _():
                ycopy(r, h).start()

    def backs(yt, lo=0, n=4):
        def b(i, _):
            m = yt * 8 + 2 * (i + lo)
            g = jnp.concatenate([Gg[m], Gg[m + 1]], axis=1)
            w = jnp.concatenate([Wp[m], Wp[m + 1]], axis=1)
            dacc[...] += lax.dot_general(w, g, TB, preferred_element_type=f32)
            return 0
        lax.fori_loop(0, n, b, 0)

    def piece(k):
        return pl.ds(pl.multiple_of(rem(z + k, 8) * 24, 8), 24)

    def scatter(i, blocks):
        v = jnp.concatenate(blocks, axis=0)
        part[i] = jnp.concatenate([v[:192], v[192:]], axis=1)
        for k in range(1, 8):
            put(part.at[i, piece(k)], part_r.at[i, k], p1S.at[i, k], p1R.at[i, k], zs[k])

    def fold_z(i):
        v = part[i, piece(0)]
        for k in range(1, 8):
            got(part_r.at[i, k], p1S.at[i, k], p1R.at[i, k])
            v = v + part_r[i, k]
        fold[i] = v
        for k in range(1, 4):
            put(fold.at[i], fold_r.at[i, k], p2S.at[i, k], p2R.at[i, k], ys[k])

    def fold_y(i):
        v = fold[i]
        for k in range(1, 4):
            got(fold_r.at[i, k], p2S.at[i, k], p2R.at[i, k])
            v = v + fold_r[i, k]
        act[i, piece(0)] = v
        mine = act.at[i, piece(0)]
        for k in range(1, 8):
            put(mine, mine, p3S.at[i, k], p3R.at[i, k], zs[k])

    def gather(i, to):
        for k in range(1, 8):
            got(act.at[i, piece(8 - k)], p3S.at[i, k], p3R.at[i, k])
        v = act[i].astype(bf16)
        to[...] = jnp.concatenate([v[:, :64], v[:, 64:]], axis=0)

    def blk(b):
        return pl.ds(128 * b, 128)

    def up_scatter():
        for k in range(1, 8):
            got(Br.at[k], bS.at[k], bR.at[k])
        scatter(1, [lax.dot_general(masked[blk(b)], Br[slot[b]], TB, preferred_element_type=f32) for b in range(3)])

    def down_scatter():
        for k in range(1, 8):
            got(Ar.at[k], aS.at[k], aR.at[k])
        scatter(0, [lax.dot_general(hid[blk(b)], Ar[slot[b]], TB, preferred_element_type=f32) for b in range(3)])

    def up_terms():
        gather(1, up_act)
        for b in range(3):
            terms[b] = lax.dot_general(up_act[blk(b)], hid[blk(b)], TA, preferred_element_type=f32).astype(bf16)
        for k in range(8):
            (Tr if k == 0 else Ts)[k] = terms[block_for(dps[k][0])]
        for k in range(1, 8):
            put(Ts.at[k], Tr.at[k], tS.at[k], tR.at[k], dps[k])

    def down_terms():
        gather(0, down_act)
        for b in range(3):
            uterms[b] = lax.dot_general(down_act[blk(b)], masked[blk(b)], TA, preferred_element_type=f32).astype(bf16)
        for k in range(8):
            (Ur if k == 0 else Us)[k] = uterms[block_for(dps[k][0])]
        for k in range(1, 8):
            put(Us.at[k], Ur.at[k], uS.at[k], uR.at[k], dps[k])

    def side():
        for b in range(3):
            dacc[:, blk(b)] += lax.dot_general(Ar[slot[b]].T, up_act[blk(b)], TB, preferred_element_type=f32)

    def owned(recv, ss, rs, to):
        for k in range(1, 8):
            got(recv.at[k], ss.at[k], rs.at[k])
        picks = [wanted(rem(dp - k + 8, 8)) for k in range(8)]
        for a in range(4):
            v = None
            for k, (found, sel) in enumerate(picks):
                w = jnp.where((found == 1) & (sel == a), 1.0, 0.0).astype(f32)
                t = w * recv[k].astype(f32)
                v = t if v is None else v + t
            to[a] = v.astype(bf16)

    loc[0].wait()
    for k in range(8):
        (Br if k == 0 else Bs)[k] = b_ref[sels[k]]
    pl.semaphore_wait(bar, len(peers))
    def first(d, i):
        put(w_hbm.at[:, pl.ds(256 * i, 256)], Wp.at[wbase + i], w1S.at[d, i], w1R.at[d, i], (XP, XM)[d])

    def came(d, i):
        got(wsl(3 if d == 0 else 1, i, 1), w1S.at[d, i], w1R.at[d, i])

    first(0, 0); first(1, 2); first(0, 1); first(1, 3)
    loc[2].wait()
    gput(0, gsl(0, 0), ZP)
    gput(1, gsl(0, 0), ZM)
    gy(0)
    for k in range(1, 8):
        put(Bs.at[k], Br.at[k], bS.at[k], bR.at[k], dps[k])
    for cp in loc[5:]:
        cp.wait()
    wput(6, 0, 0, 4, SIB)
    first(0, 2); first(1, 0); first(0, 3); first(1, 1)
    loc[1].wait()
    masked[...] = jnp.where(rows < live, grad[...], jnp.zeros_like(grad))
    loc[3].wait()
    for k in range(8):
        (Ar if k == 0 else As)[k] = a_ref[sels[k]]
    dacc[...] = jnp.zeros_like(dacc)
    loc[4].wait()
    hid[...] = hid_t[...].T

    far = rem(y - x + 4, 4)
    r1 = rem(x + jnp.where(far == 2, 1, 0), 4)
    r2 = rem(x + jnp.where(far < 2, 1, 3), 4)
    r3 = rem(x + jnp.where(far < 2, 3, far - 2), 4)
    r4 = rem(x + 2, 4)

    wgot(6, 0, 0, 4, 1)
    both(0, 0)
    gz(1); gy(1); gy(2)
    both(0, 1)
    gz(2); gy(3); gy(4)
    both(0, 2)
    gz(3); gy(5); gy(6)
    came(0, 0); wput(4, 3, 0, 1, XP); came(0, 1); wput(5, 3, 1, 1, XP); wput(7, 3, 0, 2, SIB)
    came(1, 2); wput(13, 1, 2, 1, XM); came(1, 3); wput(14, 1, 3, 1, XM); wput(9, 1, 2, 2, SIB)
    for k in range(1, 8):
        put(As.at[k], Ar.at[k], aS.at[k], aR.at[k], dps[k])
    both(0, 3)
    up_scatter()
    wgot(7, 3, 0, 2, 1); wgot(9, 1, 2, 2, 1)
    both(1, 0)
    gz(4); gy(7)
    both(0, 4)
    fold_z(1)
    both(1, 1)
    gf(0); gf(1); gf(2)
    both(1, 2)
    fold_y(1)
    gf(3); gf(4)
    both(1, 3)
    gf(5); gf(6)
    came(0, 2); came(0, 3); wput(8, 3, 2, 2, SIB)
    came(1, 0); came(1, 1); wput(10, 1, 0, 2, SIB)
    up_terms()
    wgot(8, 3, 2, 2, 1); wgot(10, 1, 0, 2, 1)
    both(2, 0)
    gf(7)
    both(1, 4)
    backs(r1)
    both(2, 1)
    backs(r2)
    both(2, 2)
    wgot(4, 2, 0, 1); wput(11, 2, 0, 1, SIB)
    wgot(13, 2, 2, 1); wput(12, 2, 2, 1, SIB)
    both(2, 3)
    wgot(5, 2, 1, 1); wput(15, 2, 1, 1, SIB)
    wgot(14, 2, 3, 1); wput(16, 2, 3, 1, SIB)
    both(2, 4)
    wgot(11, 2, 0, 1, 1); wgot(12, 2, 2, 1, 1); wgot(15, 2, 1, 1, 1); wgot(16, 2, 3, 1, 1)
    both(3, 0)
    pre(3, 1)
    for j in range(8):
        gl(j)
    backs(r3)
    level(3, 1)
    pre(3, 2)
    down_scatter()
    level(3, 2)
    fold_z(0)
    pre(3, 3)
    backs(r4, 0, 2)
    level(3, 3)
    fold_y(0)
    pre(3, 4)
    backs(r4, 2, 2)
    level(3, 4)
    down_terms()
    side()
    columns = lax.broadcasted_iota(jnp.int32, (1, 384), 1)
    dh[...] = jnp.where(columns < live, dacc[...], 0.0).astype(bf16)
    owned(Tr, tS, tR, dg)
    for b in range(3):
        acc[0, 0, blk(b)] = jnp.dot(down_act[blk(b)], Br[slot[b]], preferred_element_type=f32)
    for h in (0, 1):
        r = pl.ds(192 * h, 192)
        for j in range(3):
            got(Yr.at[j, h], yS.at[0, h], yR.at[j, h])
        t = acc[0, 0, r] + Sown[r]
        for j in range(3):
            t = t + Yr[j, h].astype(f32)
        out[r] = jnp.where(rows[192 * h:192 * h + 192] < live, t, 0.0).astype(bf16)

    owned(Ur, uS, uR, ug)
    for cp in sends:
        cp.wait_send()

    def zw(i, _):
        for h in (0, 1):
            zcopy(i // 7, rem(i, 7), h, ZP).wait_send()
        return 0
    lax.fori_loop(0, 28, zw, 0)
    for r in range(4):
        @pl.when(y != row(r, z))
        def _():
            for h in (0, 1):
                ycopy(r, h).wait_send()


def finish(a, b, c, d, oa, ob, oc, od, sems):
    cps = [pltpu.make_async_copy(i, o, sems.at[k]) for k, (i, o) in enumerate(((a, oa), (b, ob), (c, oc), (d, od)))]
    for cp in cps:
        cp.start()
    for cp in cps:
        cp.wait()


def shards(hidden, down_weight, adapter_down, adapter_up, output_grad, adapter_per_block, live_rows):
    V = pl.BlockSpec(memory_space=pltpu.VMEM)
    S = pl.BlockSpec(memory_space=pltpu.SMEM)
    A = pl.BlockSpec(memory_space=pl.ANY)
    D = pltpu.SemaphoreType.DMA
    M = pltpu.VMEM
    out, dh_t, dg_t, ug = pl.pallas_call(
        kernel,
        out_shape=(
            jax.ShapeDtypeStruct((384, 256), bf16), jax.ShapeDtypeStruct((832, 384), bf16),
            jax.ShapeDtypeStruct((4, 64, 832), bf16), jax.ShapeDtypeStruct((4, 64, 256), bf16)),
        in_specs=[S, S, A, A, A, A, A],
        out_specs=(V, V, V, V),
        scratch_shapes=[
            M((832, 384), bf16), M((384, 832), bf16), M((384, 256), bf16), M((384, 256), bf16),
            M((4, 64, 832), bf16), M((4, 64, 256), bf16),
            M((32, 832, 256), bf16),
            M((32, 384, 256), bf16),
            M((4, 7, 2, 192, 256), bf16),
            M((4, 7, 2, 192, 256), bf16),
            M((4, 2, 192, 256), bf16),
            M((3, 2, 192, 256), bf16),
            M((384, 256), f32),
            M((2, 2, 384, 256), f32),
            M((832, 384), f32),
            M((8, 64, 832), bf16), M((8, 64, 832), bf16), M((8, 64, 256), bf16), M((8, 64, 256), bf16),
            M((8, 64, 832), bf16), M((8, 64, 832), bf16), M((8, 64, 256), bf16), M((8, 64, 256), bf16),
            M((3, 64, 832), bf16), M((3, 64, 256), bf16),
            M((2, 192, 128), f32), M((2, 8, 24, 128), f32), M((2, 24, 128), f32), M((2, 4, 24, 128), f32), M((2, 192, 128), f32),
            M((384, 64), bf16), M((384, 64), bf16),
            D((9,)), D((17,)), D((17,)), D((2, 4)), D((2, 4)), D((8,)), D((8,)), D((8, 2)), D((8, 2)), D((8, 2)), D((8, 2)),
            D((4, 7, 2)), D((4, 7, 2)), D((4, 2)), D((3, 2)),
            D((8,)), D((8,)), D((8,)), D((8,)), D((8,)), D((8,)), D((8,)), D((8,)),
            D((2, 8)), D((2, 8)), D((2, 4)), D((2, 4)), D((2, 8)), D((2, 8)),
        ],
        name="layer",
        cost_estimate=pl.CostEstimate(flops=2 * 2 * 384 * 832 * 8192, bytes_accessed=6 * 2 ** 20, transcendentals=0),
        compiler_params=pltpu.CompilerParams(collective_id=0, has_side_effects=True, vmem_limit_bytes=58 * 2 ** 20),
    )(adapter_per_block, live_rows, hidden.T, down_weight, jnp.swapaxes(adapter_down, 1, 2), adapter_up, output_grad)
    parts = (out, dh_t, dg_t, ug)
    out, dh_t, dg_t, ug = pl.pallas_call(
        finish,
        out_shape=tuple(jax.ShapeDtypeStruct(v.shape, v.dtype) for v in parts),
        in_specs=[A] * 4, out_specs=(A,) * 4, scratch_shapes=[D((4,))], name="finish",
        cost_estimate=pl.CostEstimate(flops=0, bytes_accessed=4 * 2 ** 20, transcendentals=0),
    )(*parts)
    return out, dh_t.T, jnp.swapaxes(dg_t, 1, 2), ug


def solution(mesh):
    return jax.shard_map(
        shards,
        mesh=mesh,
        in_specs=(P("dp", "mp"), P("mp", "dp"), P("dp", "mp", None), P("dp", None, "mp"), P("dp", "mp"), P(), P()),
        out_specs=(P("dp", "mp"), P("dp", "mp"), P("dp", "mp", None), P("dp", None, "mp")),
        check_vma=False,
    )
```

```python
import jax
import jax.numpy as jnp
from jax import lax
from jax.experimental import pallas as pl
from jax.experimental.pallas import tpu as pltpu
from jax.sharding import PartitionSpec as P

BLK = 128
MESH = pl.DeviceIdType.MESH
f32, bf16 = jnp.float32, jnp.bfloat16
TB = (((1,), (1,)), ((), ()))
TA = (((0,), (0,)), ((), ()))


def rem(a, n):
    return lax.rem(a, n)


def kernel(ids, lives, hid_h, w_hbm, a_h, b_h, grad_h, out_h, dh_h, dg_h, ug_h, out, dh, dg, ug, oS,
           hid_t, hid, grad, masked, a_ref, b_ref, Wp, Gg, Zs, Zr, Ys, Yr, Sown, acc, dacc,
           As, Ar, Bs, Br, Ts, Tr, Us, Ur, terms, uterms, part, part_r, fold, fold_r, act, down_act, up_act,
           lS, wS, wR, w1S, w1R, gS, gR, gyS, gyR, gfS, gfR, zS, zR, yS, yR,
           aS, aR, bS, bR, tS, tR, uS, uR, p1S, p1R, p2S, p2R, p3S, p3R):
    dp, mp = lax.axis_index("dp"), lax.axis_index("mp")
    x, c, y, z = dp // 2, rem(dp, 2), mp // 8, rem(mp, 8)

    def dev(dx=0, dc=0, dy=0, dz=0):
        return (rem(x + dx, 4) * 2 + rem(c + dc, 2), rem(y + dy, 4) * 8 + rem(z + dz, 8))

    XP, XM, SIB = dev(dx=1), dev(dx=3), dev(dc=1)
    dps = [(rem(dp + k, 8), mp) for k in range(8)]
    ys = [dev(dy=k) for k in range(4)]
    zs = [dev(dz=k) for k in range(8)]
    YP, YM, ZP, ZM = ys[1], ys[3], zs[1], zs[7]

    bar = pltpu.get_barrier_semaphore()
    peers = dps[1:] + ys[1:] + zs[1:]
    for p in peers:
        pl.semaphore_signal(bar, inc=1, device_id=p, device_id_type=MESH)

    wbase = x * 8 + c * 4
    loc = [pltpu.make_async_copy(s, d, lS.at[i]) for i, (s, d) in enumerate(
        [(b_h, b_ref), (grad_h, grad), (grad_h, Gg.at[y * 8 + z]), (a_h, a_ref), (hid_h, hid_t)]
        + [(w_hbm.at[:, pl.ds(256 * i, 256)], Wp.at[wbase + i]) for i in range(4)])]
    for cp in loc:
        cp.start()

    def wanted(d):
        found, sel = jnp.int32(0), jnp.int32(0)
        for b in range(3):
            i = ids[3 * d + b]
            hit = (i // 4) == dp
            found = jnp.where(hit, 1, found)
            sel = jnp.where(hit, i % 4, sel)
        return found, sel

    def block_for(o):
        sel = jnp.int32(0)
        for b in range(1, 3):
            sel = jnp.where(own[b] == o, b, sel)
        return sel


    sends = []

    def put(src, dst, ss, rs, to, record=True):
        cp = pltpu.make_async_remote_copy(src_ref=src, dst_ref=dst, send_sem=ss, recv_sem=rs, device_id=to, device_id_type=MESH)
        cp.start()
        if record:
            sends.append(cp)

    def left(ref, ss):
        pltpu.make_async_remote_copy(src_ref=ref, dst_ref=ref, send_sem=ss, recv_sem=ss, device_id=XP, device_id_type=MESH).wait_send()

    def got(dst, ss, rs):
        pltpu.make_async_remote_copy(src_ref=dst, dst_ref=dst, send_sem=ss, recv_sem=rs, device_id=XP, device_id_type=MESH).wait_recv()

    def wsl(dx, i, n, dc=0):
        return Wp.at[pl.ds(rem(x + dx, 4) * 8 + rem(c + dc, 2) * 4 + i, n)]

    def wput(k, dx, i, n, to):
        put(wsl(dx, i, n), wsl(dx, i, n), wS.at[k], wR.at[k], to)

    def wgot(k, dx, i, n, dc=0):
        got(wsl(dx, i, n, dc), wS.at[k], wR.at[k])

    ORDER = (0, 7, 1, 6, 2, 5, 3, 4)

    def gsl(dy, dz, lo=0, n=384):
        return Gg.at[rem(y + dy, 4) * 8 + rem(z + dz, 8), pl.ds(lo, n)]

    def gput(k, ref, to):
        put(ref, ref, gS.at[k], gR.at[k], to)

    def gz(k):
        if k < 4:
            lo, hi = gsl(0, 8 - k), gsl(0, k)
            got(lo, gS.at[2 * k - 2], gR.at[2 * k - 2])
            got(hi, gS.at[2 * k - 1], gR.at[2 * k - 1])
            if k == 3:
                lo, hi = gsl(0, 5, 0, 192), gsl(0, 3, 192, 192)
            gput(2 * k, lo, ZP)
            gput(2 * k + 1, hi, ZM)
        else:
            got(gsl(0, 4, 0, 192), gS.at[6], gR.at[6])
            got(gsl(0, 4, 192, 192), gS.at[7], gR.at[7])

    def gy(j):
        ref = gsl(0, ORDER[j])
        put(ref, ref, gyS.at[0], gyR.at[j, 0], YP, False)
        put(ref, ref, gyS.at[0], gyR.at[j, 1], YM, False)

    def gf(j):
        got(gsl(3, ORDER[j]), gyS.at[0], gyR.at[j, 0])
        ref = gsl(3, ORDER[j], 0, 192)
        put(ref, ref, gfS.at[0], gfR.at[0], YP, False)
        got(gsl(1, ORDER[j]), gyS.at[0], gyR.at[j, 1])
        ref = gsl(1, ORDER[j], 192, 192)
        put(ref, ref, gfS.at[0], gfR.at[0], YM, False)

    def gl():
        got(Gg.at[pl.ds(rem(y + 2, 4) * 8, 8)], gfS.at[0], gfR.at[0])

    def row(r, zt):
        if r in (0, 3):
            return rem(x + (0 if r == 0 else 2), 4)
        left = rem(zt, 4) < 2
        return rem(x + jnp.where(left, 3, 1) if r == 1 else x + jnp.where(left, 1, 3), 4)

    def pre(r, level):
        b = r // 3
        if level in (0, 4):
            zt = rem(z + 4, 8) if level == 0 else z
            acc[b, 0] = jnp.dot(hid[...], Wp[row(r, zt) * 8 + zt], preferred_element_type=f32)
            return
        for s in (0, 1):
            zt = rem(z + (4 + level if s == 0 else 4 - level), 8)
            acc[b, s] = jnp.dot(hid[...], Wp[row(r, zt) * 8 + zt], preferred_element_type=f32)

    def zcopy(r, k, h, to):
        return pltpu.make_async_remote_copy(
            src_ref=Zs.at[r, k, h], dst_ref=Zr.at[r, k, h], send_sem=zS.at[r],
            recv_sem=zR.at[r, k, h], device_id=to, device_id_type=MESH)

    def half(r, s, h):
        return acc[r // 3, s, pl.ds(192 * h, 192)]

    def send(r, k, h, to, v):
        Zs[r, k, h] = v.astype(bf16)
        zcopy(r, k, h, to).start()

    def level0(r):
        for h, to in ((0, ZM), (1, ZP)):
            send(r, 0, h, to, half(r, 0, h))

    def level1(r):
        for s, to in ((0, ZM), (1, ZP)):
            send(r, 1 + s, 1 - s, to, half(r, s, 1 - s))
        for s, to in ((0, ZM), (1, ZP)):
            zcopy(r, 0, s, to).wait_recv()
            send(r, 1 + s, s, to, half(r, s, s) + Zr[r, 0, s].astype(f32))

    def level23(r, l):
        for i in (0, 1):
            for s, to in ((0, ZM), (1, ZP)):
                k, h = 2 * l - 1 + s, (1 - s if i == 0 else s)
                zcopy(r, k - 2, h, to).wait_recv()
                send(r, k, h, to, half(r, s, h) + Zr[r, k - 2, h].astype(f32))

    def level(r, l):
        if l == 0:
            level0(r)
        elif l == 1:
            level1(r)
        elif l < 4:
            level23(r, l)
        else:
            level4(r)

    def both(r, l):
        pre(r, l)
        level(r, l)

    def ycopy(r, h):
        yt = row(r, z)
        j = rem(y - yt + 4, 4)
        return pltpu.make_async_remote_copy(
            src_ref=Ys.at[r, h], dst_ref=Yr.at[j - 1, h], send_sem=yS.at[r, h], recv_sem=yR.at[j - 1, h],
            device_id=(dp, yt * 8 + z), device_id_type=MESH)

    def level4(r):
        for h in (0, 1):
            for k in (5, 6):
                zcopy(r, k, h, ZP).wait_recv()
            v = half(r, 0, h) + (Zr[r, 5, h].astype(f32) + Zr[r, 6, h].astype(f32))
            Ys[r, h] = v.astype(bf16)

            @pl.when(y == row(r, z))
            def _():
                Sown[pl.ds(192 * h, 192)] = v

            @pl.when(y != row(r, z))
            def _():
                ycopy(r, h).start()

    def backs(yt, lo=0, n=4):
        def b(i, _):
            m = yt * 8 + 2 * (i + lo)
            g = jnp.concatenate([Gg[m], Gg[m + 1]], axis=1)
            w = jnp.concatenate([Wp[m], Wp[m + 1]], axis=1)
            dacc[...] += lax.dot_general(w, g, TB, preferred_element_type=f32)
            return 0
        lax.fori_loop(0, n, b, 0)

    def piece(k):
        return pl.ds(pl.multiple_of(rem(z + k, 8) * 24, 8), 24)

    def scatter(i, blocks):
        v = jnp.concatenate(blocks, axis=0)
        part[i] = jnp.concatenate([v[:192], v[192:]], axis=1)
        for k in range(1, 8):
            put(part.at[i, piece(k)], part_r.at[i, k], p1S.at[i], p1R.at[i], zs[k], False)

    def fold_z(i):
        v = part[i, piece(0)]
        got(part_r.at[i, pl.ds(1, 7)], p1S.at[i], p1R.at[i])
        for k in range(1, 8):
            v = v + part_r[i, k]
        fold[i] = v
        for k in range(1, 4):
            put(fold.at[i], fold_r.at[i, k], p2S.at[i], p2R.at[i], ys[k], False)

    def fold_y(i):
        v = fold[i]
        got(fold_r.at[i, pl.ds(1, 3)], p2S.at[i], p2R.at[i])
        for k in range(1, 4):
            v = v + fold_r[i, k]
        act[i, piece(0)] = v
        mine = act.at[i, piece(0)]
        for k in range(1, 8):
            put(mine, mine, p3S.at[i], p3R.at[i], zs[k], False)

    def gather(i, to):
        got(act.at[i, pl.ds(0, 168)], p3S.at[i], p3R.at[i])
        v = act[i].astype(bf16)
        to[...] = jnp.concatenate([v[:, :64], v[:, 64:]], axis=0)

    def blk(b):
        return pl.ds(128 * b, 128)

    def up_scatter():
        got(Br.at[pl.ds(1, 7)], bS.at[0], bR.at[0])
        scatter(1, [lax.dot_general(masked[blk(b)], Br[slot[b]], TB, preferred_element_type=f32) for b in range(3)])

    def down_scatter():
        got(Ar.at[pl.ds(1, 7)], aS.at[0], aR.at[0])
        scatter(0, [lax.dot_general(hid[blk(b)], Ar[slot[b]], TB, preferred_element_type=f32) for b in range(3)])

    def up_terms():
        gather(1, up_act)
        for b in range(3):
            terms[b] = lax.dot_general(up_act[blk(b)], hid[blk(b)], TA, preferred_element_type=f32).astype(bf16)
        for k in range(8):
            (Tr if k == 0 else Ts)[k] = terms[block_for(dps[k][0])]
        for k in range(1, 8):
            put(Ts.at[k], Tr.at[k], tS.at[0], tR.at[0], dps[k], False)

    def down_terms():
        gather(0, down_act)
        for b in range(3):
            uterms[b] = lax.dot_general(down_act[blk(b)], masked[blk(b)], TA, preferred_element_type=f32).astype(bf16)
        for k in range(8):
            (Ur if k == 0 else Us)[k] = uterms[block_for(dps[k][0])]
        for k in range(1, 8):
            put(Us.at[k], Ur.at[k], uS.at[0], uR.at[0], dps[k], False)

    def side():
        for b in range(3):
            dacc[:, blk(b)] += lax.dot_general(Ar[slot[b]].T, up_act[blk(b)], TB, preferred_element_type=f32)

    def owned(recv, ss, rs, to):
        got(recv.at[pl.ds(1, 7)], ss.at[0], rs.at[0])
        picks = [wanted(rem(dp - k + 8, 8)) for k in range(8)]
        for a in range(4):
            v = None
            for k, (found, sel) in enumerate(picks):
                w = jnp.where((found == 1) & (sel == a), 1.0, 0.0).astype(f32)
                t = w * recv[k].astype(f32)
                v = t if v is None else v + t
            to[a] = v.astype(bf16)

    pl.semaphore_wait(bar, len(peers))
    def first(d, i):
        put(w_hbm.at[:, pl.ds(256 * i, 256)], Wp.at[wbase + i], w1S.at[d, i], w1R.at[d, i], (XP, XM)[d])

    def came(d, i):
        got(wsl(3 if d == 0 else 1, i, 1), w1S.at[d, i], w1R.at[d, i])

    first(0, 0); first(1, 2); first(0, 1); first(1, 3)
    loc[2].wait()
    gput(0, gsl(0, 0), ZP)
    gput(1, gsl(0, 0), ZM)
    gy(0)
    live = lives[dp]
    rows = lax.broadcasted_iota(jnp.int32, (384, 1), 0)
    own = [ids[3 * dp + b] // 4 for b in range(3)]
    slot = [rem(dp - own[b] + 8, 8) for b in range(3)]
    sels = [wanted(dps[k][0])[1] for k in range(8)]
    loc[0].wait()
    for k in range(8):
        (Br if k == 0 else Bs)[k] = b_ref[sels[k]]
    for k in range(1, 8):
        put(Bs.at[k], Br.at[k], bS.at[0], bR.at[0], dps[k], False)
    for cp in loc[5:]:
        cp.wait()
    wput(6, 0, 0, 4, SIB)
    first(0, 2); first(1, 0); first(0, 3); first(1, 1)
    loc[1].wait()
    masked[...] = jnp.where(rows < live, grad[...], jnp.zeros_like(grad))
    loc[3].wait()
    for k in range(8):
        (Ar if k == 0 else As)[k] = a_ref[sels[k]]
    dacc[...] = jnp.zeros_like(dacc)
    loc[4].wait()
    hid[...] = hid_t[...].T

    far = rem(y - x + 4, 4)
    r1 = rem(x + jnp.where(far == 2, 1, 0), 4)
    r2 = rem(x + jnp.where(far < 2, 1, 3), 4)
    r3 = rem(x + jnp.where(far < 2, 3, far - 2), 4)
    r4 = rem(x + 2, 4)

    wgot(6, 0, 0, 4, 1)
    both(0, 0)
    gz(1); gy(1); gy(2)
    both(0, 1)
    gz(2); gy(3); gy(4)
    both(0, 2)
    gz(3); gy(5); gy(6)
    came(0, 0); wput(4, 3, 0, 1, XP); came(0, 1); wput(5, 3, 1, 1, XP); wput(7, 3, 0, 2, SIB)
    came(1, 2); wput(13, 1, 2, 1, XM); came(1, 3); wput(14, 1, 3, 1, XM); wput(9, 1, 2, 2, SIB)
    for k in range(1, 8):
        put(As.at[k], Ar.at[k], aS.at[0], aR.at[0], dps[k], False)
    both(0, 3)
    up_scatter()
    wgot(7, 3, 0, 2, 1); wgot(9, 1, 2, 2, 1)
    both(1, 0)
    gz(4); gy(7)
    both(0, 4)
    fold_z(1)
    both(1, 1)
    gf(0); gf(1); gf(2)
    both(1, 2)
    fold_y(1)
    gf(3); gf(4)
    both(1, 3)
    gf(5); gf(6)
    came(0, 2); came(0, 3); wput(8, 3, 2, 2, SIB)
    came(1, 0); came(1, 1); wput(10, 1, 0, 2, SIB)
    up_terms()
    wgot(8, 3, 2, 2, 1); wgot(10, 1, 0, 2, 1)
    both(2, 0)
    gf(7)
    both(1, 4)
    backs(r1)
    both(2, 1)
    backs(r2)
    both(2, 2)
    for cp in sends:
        cp.wait_send()
    sends.clear()
    left(Bs.at[pl.ds(1, 7)], bS.at[0])
    left(part.at[1, pl.ds(0, 168)], p1S.at[1])
    left(fold_r.at[1, pl.ds(1, 3)], p2S.at[1])
    left(part.at[1, pl.ds(0, 168)], p3S.at[1])
    left(Gg.at[pl.ds(0, 16)], gyS.at[0])
    left(Zs.at[0], zS.at[0])
    left(Zs.at[1], zS.at[1])
    wgot(4, 2, 0, 1); wput(11, 2, 0, 1, SIB)
    wgot(13, 2, 2, 1); wput(12, 2, 2, 1, SIB)
    both(2, 3)
    wgot(5, 2, 1, 1); wput(15, 2, 1, 1, SIB)
    wgot(14, 2, 3, 1); wput(16, 2, 3, 1, SIB)
    both(2, 4)
    wgot(11, 2, 0, 1, 1); wgot(12, 2, 2, 1, 1); wgot(15, 2, 1, 1, 1); wgot(16, 2, 3, 1, 1)
    both(3, 0)
    pre(3, 1)
    gl()
    left(Gg.at[pl.ds(0, 8)], gfS.at[0])
    backs(r3)
    level(3, 1)
    pre(3, 2)
    down_scatter()
    level(3, 2)
    fold_z(0)
    pre(3, 3)
    backs(r4, 0, 2)
    level(3, 3)
    fold_y(0)
    left(As.at[pl.ds(1, 7)], aS.at[0])
    pre(3, 4)
    backs(r4, 2, 2)
    level(3, 4)
    down_terms()
    side()
    columns = lax.broadcasted_iota(jnp.int32, (1, 384), 1)
    dh[...] = jnp.where(columns < live, dacc[...], 0.0).astype(bf16)
    outs = [pltpu.make_async_copy(s, d, oS.at[i]) for i, (s, d) in enumerate(((out, out_h), (dh, dh_h), (dg, dg_h), (ug, ug_h)))]
    outs[1].start()
    owned(Tr, tS, tR, dg)
    outs[2].start()
    for b in range(3):
        acc[0, 0, blk(b)] = jnp.dot(down_act[blk(b)], Br[slot[b]], preferred_element_type=f32)
    for h in (0, 1):
        r = pl.ds(192 * h, 192)
        for j in range(3):
            got(Yr.at[j, h], yS.at[0, h], yR.at[j, h])
        t = acc[0, 0, r] + Sown[r]
        for j in range(3):
            t = t + Yr[j, h].astype(f32)
        out[r] = jnp.where(rows[192 * h:192 * h + 192] < live, t, 0.0).astype(bf16)

    outs[0].start()
    owned(Ur, uS, uR, ug)
    outs[3].start()
    for cp in sends:
        cp.wait_send()
    left(Us.at[pl.ds(1, 7)], uS.at[0])
    left(Ts.at[pl.ds(1, 7)], tS.at[0])
    left(part.at[0, pl.ds(0, 168)], p1S.at[0])
    left(fold_r.at[0, pl.ds(1, 3)], p2S.at[0])
    left(part.at[0, pl.ds(0, 168)], p3S.at[0])
    left(Zs.at[2], zS.at[2])
    left(Zs.at[3], zS.at[3])
    for r in range(4):
        @pl.when(y != row(r, z))
        def _():
            for h in (0, 1):
                ycopy(r, h).wait_send()
    for cp in outs:
        cp.wait()


def finish(a, b, c, d, oa, ob, oc, od):
    for i, o in ((a, oa), (b, ob), (c, oc), (d, od)):
        o[...] = i[...]


def shards(hidden, down_weight, adapter_down, adapter_up, output_grad, adapter_per_block, live_rows):
    V = pl.BlockSpec(memory_space=pltpu.VMEM)
    S = pl.BlockSpec(memory_space=pltpu.SMEM)
    A = pl.BlockSpec(memory_space=pl.ANY)
    D = pltpu.SemaphoreType.DMA
    M = pltpu.VMEM
    out, dh_t, dg_t, ug = pl.pallas_call(
        kernel,
        out_shape=(
            jax.ShapeDtypeStruct((384, 256), bf16), jax.ShapeDtypeStruct((832, 384), bf16),
            jax.ShapeDtypeStruct((4, 64, 832), bf16), jax.ShapeDtypeStruct((4, 64, 256), bf16)),
        in_specs=[S, S, A, A, A, A, A],
        out_specs=(A, A, A, A),
        scratch_shapes=[
            M((384, 256), bf16), M((832, 384), bf16), M((4, 64, 832), bf16), M((4, 64, 256), bf16), D((4,)),
            M((832, 384), bf16), M((384, 832), bf16), M((384, 256), bf16), M((384, 256), bf16),
            M((4, 64, 832), bf16), M((4, 64, 256), bf16),
            M((32, 832, 256), bf16),
            M((32, 384, 256), bf16),
            M((4, 7, 2, 192, 256), bf16),
            M((4, 7, 2, 192, 256), bf16),
            M((4, 2, 192, 256), bf16),
            M((3, 2, 192, 256), bf16),
            M((384, 256), f32),
            M((2, 2, 384, 256), f32),
            M((832, 384), f32),
            M((8, 64, 832), bf16), M((8, 64, 832), bf16), M((8, 64, 256), bf16), M((8, 64, 256), bf16),
            M((8, 64, 832), bf16), M((8, 64, 832), bf16), M((8, 64, 256), bf16), M((8, 64, 256), bf16),
            M((3, 64, 832), bf16), M((3, 64, 256), bf16),
            M((2, 192, 128), f32), M((2, 8, 24, 128), f32), M((2, 24, 128), f32), M((2, 4, 24, 128), f32), M((2, 192, 128), f32),
            M((384, 64), bf16), M((384, 64), bf16),
            D((9,)), D((17,)), D((17,)), D((2, 4)), D((2, 4)), D((8,)), D((8,)), D((1,)), D((8, 2)), D((1,)), D((1,)),
            D((4,)), D((4, 7, 2)), D((4, 2)), D((3, 2)),
            D((1,)), D((1,)), D((1,)), D((1,)), D((1,)), D((1,)), D((1,)), D((1,)),
            D((2,)), D((2,)), D((2,)), D((2,)), D((2,)), D((2,)),
        ],
        name="layer",
        cost_estimate=pl.CostEstimate(flops=2 * 2 * 384 * 832 * 8192, bytes_accessed=6 * 2 ** 20, transcendentals=0),
        compiler_params=pltpu.CompilerParams(collective_id=0, has_side_effects=True, vmem_limit_bytes=58 * 2 ** 20),
    )(adapter_per_block, live_rows, hidden.T, down_weight, jnp.swapaxes(adapter_down, 1, 2), adapter_up, output_grad)
    parts = (out, dh_t, dg_t, ug)
    out, dh_t, dg_t, ug = pl.pallas_call(
        finish,
        out_shape=tuple(jax.ShapeDtypeStruct(v.shape, v.dtype) for v in parts),
        in_specs=[V] * 4, out_specs=(V,) * 4, name="finish",
        cost_estimate=pl.CostEstimate(flops=0, bytes_accessed=4 * 2 ** 20, transcendentals=0),
    )(*parts)
    return out, dh_t.T, jnp.swapaxes(dg_t, 1, 2), ug


def solution(mesh):
    return jax.shard_map(
        shards,
        mesh=mesh,
        in_specs=(P("dp", "mp"), P("mp", "dp"), P("dp", "mp", None), P("dp", None, "mp"), P("dp", "mp"), P(), P()),
        out_specs=(P("dp", "mp"), P("dp", "mp"), P("dp", "mp", None), P("dp", None, "mp")),
        check_vma=False,
    )
```

```python
import jax
import jax.numpy as jnp
from jax import lax
from jax.experimental import pallas as pl
from jax.experimental.pallas import tpu as pltpu
from jax.sharding import PartitionSpec as P

BLK = 128
MESH = pl.DeviceIdType.MESH
f32, bf16 = jnp.float32, jnp.bfloat16
TB = (((1,), (1,)), ((), ()))
TA = (((0,), (0,)), ((), ()))


def rem(a, n):
    return lax.rem(a, n)


def kernel(ids, lives, hid_h, w_hbm, a_h, b_h, grad_h, out_h, dh_h, dg_h, ug_h, out, dh, dg, ug, oS,
           hid_t, hid, grad, masked, a_ref, b_ref, Wp, Gg, Zs, Zr, Ys, Yr, Sown, acc, dacc,
           As, Ar, Bs, Br, Ts, Tr, Us, Ur, terms, uterms, part, part_r, fold, fold_r, act, down_act, up_act,
           lS, wS, wR, w1S, w1R, gS, gR, gyS, gyR, gfS, gfR, zS, zR, yS, yR,
           aS, aR, bS, bR, tS, tR, uS, uR, p1S, p1R, p2S, p2R, p3S, p3R):
    dp, mp = lax.axis_index("dp"), lax.axis_index("mp")
    x, c, y, z = dp // 2, rem(dp, 2), mp // 8, rem(mp, 8)

    def dev(dx=0, dc=0, dy=0, dz=0):
        return (rem(x + dx, 4) * 2 + rem(c + dc, 2), rem(y + dy, 4) * 8 + rem(z + dz, 8))

    XP, XM, SIB = dev(dx=1), dev(dx=3), dev(dc=1)
    dps = [(rem(dp + k, 8), mp) for k in range(8)]
    ys = [dev(dy=k) for k in range(4)]
    zs = [dev(dz=k) for k in range(8)]
    YP, YM, ZP, ZM = ys[1], ys[3], zs[1], zs[7]

    bar = pltpu.get_barrier_semaphore()
    peers = dps[1:] + ys[1:] + zs[1:]
    for p in peers:
        pl.semaphore_signal(bar, inc=1, device_id=p, device_id_type=MESH)

    wbase = x * 8 + c * 4
    loc = [pltpu.make_async_copy(s, d, lS.at[i]) for i, (s, d) in enumerate(
        [(b_h, b_ref), (grad_h, grad), (grad_h, Gg.at[y * 8 + z]), (a_h, a_ref), (hid_h, hid_t)]
        + [(w_hbm.at[:, pl.ds(256 * i, 256)], Wp.at[wbase + i]) for i in range(4)])]
    for cp in loc:
        cp.start()

    def wanted(d):
        found, sel = jnp.int32(0), jnp.int32(0)
        for b in range(3):
            i = ids[3 * d + b]
            hit = (i // 4) == dp
            found = jnp.where(hit, 1, found)
            sel = jnp.where(hit, i % 4, sel)
        return found, sel

    def block_for(o):
        sel = jnp.int32(0)
        for b in range(1, 3):
            sel = jnp.where(own[b] == o, b, sel)
        return sel


    sends = []

    def put(src, dst, ss, rs, to, record=True):
        cp = pltpu.make_async_remote_copy(src_ref=src, dst_ref=dst, send_sem=ss, recv_sem=rs, device_id=to, device_id_type=MESH)
        cp.start()
        if record:
            sends.append(cp)

    def left(ref, ss):
        pltpu.make_async_remote_copy(src_ref=ref, dst_ref=ref, send_sem=ss, recv_sem=ss, device_id=XP, device_id_type=MESH).wait_send()

    def got(dst, ss, rs):
        pltpu.make_async_remote_copy(src_ref=dst, dst_ref=dst, send_sem=ss, recv_sem=rs, device_id=XP, device_id_type=MESH).wait_recv()

    def wsl(dx, i, n, dc=0):
        return Wp.at[pl.ds(rem(x + dx, 4) * 8 + rem(c + dc, 2) * 4 + i, n)]

    def wput(k, dx, i, n, to):
        put(wsl(dx, i, n), wsl(dx, i, n), wS.at[k], wR.at[k], to)

    def wgot(k, dx, i, n, dc=0):
        got(wsl(dx, i, n, dc), wS.at[k], wR.at[k])

    ORDER = (0, 7, 1, 6, 2, 5, 3, 4)

    def gsl(dy, dz, lo=0, n=384):
        return Gg.at[rem(y + dy, 4) * 8 + rem(z + dz, 8), pl.ds(lo, n)]

    def gput(k, ref, to):
        put(ref, ref, gS.at[k], gR.at[k], to)

    def gz(k):
        if k < 4:
            lo, hi = gsl(0, 8 - k), gsl(0, k)
            got(lo, gS.at[2 * k - 2], gR.at[2 * k - 2])
            got(hi, gS.at[2 * k - 1], gR.at[2 * k - 1])
            if k == 3:
                lo, hi = gsl(0, 5, 0, 192), gsl(0, 3, 192, 192)
            gput(2 * k, lo, ZP)
            gput(2 * k + 1, hi, ZM)
        else:
            got(gsl(0, 4, 0, 192), gS.at[6], gR.at[6])
            got(gsl(0, 4, 192, 192), gS.at[7], gR.at[7])

    def gy(j):
        ref = gsl(0, ORDER[j])
        put(ref, ref, gyS.at[0], gyR.at[j, 0], YP, False)
        put(ref, ref, gyS.at[0], gyR.at[j, 1], YM, False)

    def gf(j):
        got(gsl(3, ORDER[j]), gyS.at[0], gyR.at[j, 0])
        ref = gsl(3, ORDER[j], 0, 192)
        put(ref, ref, gfS.at[0], gfR.at[0], YP, False)
        got(gsl(1, ORDER[j]), gyS.at[0], gyR.at[j, 1])
        ref = gsl(1, ORDER[j], 192, 192)
        put(ref, ref, gfS.at[0], gfR.at[0], YM, False)

    def gl():
        got(Gg.at[pl.ds(rem(y + 2, 4) * 8, 8)], gfS.at[0], gfR.at[0])

    def row(r, zt):
        if r in (0, 3):
            return rem(x + (0 if r == 0 else 2), 4)
        left = rem(zt, 4) < 2
        return rem(x + jnp.where(left, 3, 1) if r == 1 else x + jnp.where(left, 1, 3), 4)

    def pre(r, level):
        b = r // 3
        if level in (0, 4):
            zt = rem(z + 4, 8) if level == 0 else z
            acc[b, 0] = jnp.dot(hid[...], Wp[row(r, zt) * 8 + zt], preferred_element_type=f32)
            return
        for s in (0, 1):
            zt = rem(z + (4 + level if s == 0 else 4 - level), 8)
            acc[b, s] = jnp.dot(hid[...], Wp[row(r, zt) * 8 + zt], preferred_element_type=f32)

    def zcopy(r, k, h, to):
        return pltpu.make_async_remote_copy(
            src_ref=Zs.at[r, k, h], dst_ref=Zr.at[r, k, h], send_sem=zS.at[r],
            recv_sem=zR.at[r, k, h], device_id=to, device_id_type=MESH)

    def half(r, s, h):
        return acc[r // 3, s, pl.ds(192 * h, 192)]

    def send(r, k, h, to, v):
        Zs[r, k, h] = v.astype(bf16)
        zcopy(r, k, h, to).start()

    def level0(r):
        for h, to in ((0, ZM), (1, ZP)):
            send(r, 0, h, to, half(r, 0, h))

    def level1(r):
        for s, to in ((0, ZM), (1, ZP)):
            send(r, 1 + s, 1 - s, to, half(r, s, 1 - s))
        for s, to in ((0, ZM), (1, ZP)):
            zcopy(r, 0, s, to).wait_recv()
            send(r, 1 + s, s, to, half(r, s, s) + Zr[r, 0, s].astype(f32))

    def level23(r, l):
        for i in (0, 1):
            for s, to in ((0, ZM), (1, ZP)):
                k, h = 2 * l - 1 + s, (1 - s if i == 0 else s)
                zcopy(r, k - 2, h, to).wait_recv()
                send(r, k, h, to, half(r, s, h) + Zr[r, k - 2, h].astype(f32))

    def level(r, l):
        if l == 0:
            level0(r)
        elif l == 1:
            level1(r)
        elif l < 4:
            level23(r, l)
        else:
            level4(r)

    def both(r, l):
        pre(r, l)
        level(r, l)

    def ycopy(r, h):
        yt = row(r, z)
        j = rem(y - yt + 4, 4)
        return pltpu.make_async_remote_copy(
            src_ref=Ys.at[r, h], dst_ref=Yr.at[j - 1, h], send_sem=yS.at[r, h], recv_sem=yR.at[j - 1, h],
            device_id=(dp, yt * 8 + z), device_id_type=MESH)

    def level4(r):
        for h in (0, 1):
            for k in (5, 6):
                zcopy(r, k, h, ZP).wait_recv()
            v = half(r, 0, h) + (Zr[r, 5, h].astype(f32) + Zr[r, 6, h].astype(f32))
            Ys[r, h] = v.astype(bf16)

            @pl.when(y == row(r, z))
            def _():
                Sown[pl.ds(192 * h, 192)] = v

            @pl.when(y != row(r, z))
            def _():
                ycopy(r, h).start()

    def backs(yt, lo=0, n=4):
        def b(i, _):
            m = yt * 8 + 2 * (i + lo)
            g = jnp.concatenate([Gg[m], Gg[m + 1]], axis=1)
            w = jnp.concatenate([Wp[m], Wp[m + 1]], axis=1)
            dacc[...] += lax.dot_general(w, g, TB, preferred_element_type=f32)
            return 0
        lax.fori_loop(0, n, b, 0)

    def piece(k):
        return pl.ds(pl.multiple_of(rem(z + k, 8) * 24, 8), 24)

    def scatter(i, blocks):
        v = jnp.concatenate(blocks, axis=0)
        part[i] = jnp.concatenate([v[:192], v[192:]], axis=1)
        for k in range(1, 8):
            put(part.at[i, piece(k)], part_r.at[i, k], p1S.at[i], p1R.at[i], zs[k], False)

    def fold_z(i):
        v = part[i, piece(0)]
        got(part_r.at[i, pl.ds(1, 7)], p1S.at[i], p1R.at[i])
        for k in range(1, 8):
            v = v + part_r[i, k]
        fold[i] = v
        for k in range(1, 4):
            put(fold.at[i], fold_r.at[i, k], p2S.at[i], p2R.at[i], ys[k], False)

    def fold_y(i):
        v = fold[i]
        got(fold_r.at[i, pl.ds(1, 3)], p2S.at[i], p2R.at[i])
        for k in range(1, 4):
            v = v + fold_r[i, k]
        act[i, piece(0)] = v
        mine = act.at[i, piece(0)]
        for k in range(1, 8):
            put(mine, mine, p3S.at[i], p3R.at[i], zs[k], False)

    def gather(i, to):
        got(act.at[i, pl.ds(0, 168)], p3S.at[i], p3R.at[i])
        v = act[i].astype(bf16)
        to[...] = jnp.concatenate([v[:, :64], v[:, 64:]], axis=0)

    def blk(b):
        return pl.ds(128 * b, 128)

    def up_scatter():
        got(Br.at[pl.ds(1, 7)], bS.at[0], bR.at[0])
        scatter(1, [lax.dot_general(masked[blk(b)], Br[slot[b]], TB, preferred_element_type=f32) for b in range(3)])

    def down_scatter():
        got(Ar.at[pl.ds(1, 7)], aS.at[0], aR.at[0])
        scatter(0, [lax.dot_general(hid[blk(b)], Ar[slot[b]], TB, preferred_element_type=f32) for b in range(3)])

    def up_terms():
        gather(1, up_act)
        for b in range(3):
            terms[b] = lax.dot_general(up_act[blk(b)], hid[blk(b)], TA, preferred_element_type=f32).astype(bf16)
        for k in range(8):
            (Tr if k == 0 else Ts)[k] = terms[block_for(dps[k][0])]
        for k in range(1, 8):
            put(Ts.at[k], Tr.at[k], tS.at[0], tR.at[0], dps[k], False)

    def down_terms():
        gather(0, down_act)
        for b in range(3):
            uterms[b] = lax.dot_general(down_act[blk(b)], masked[blk(b)], TA, preferred_element_type=f32).astype(bf16)
        for k in range(8):
            (Ur if k == 0 else Us)[k] = uterms[block_for(dps[k][0])]
        for k in range(1, 8):
            put(Us.at[k], Ur.at[k], uS.at[0], uR.at[0], dps[k], False)

    def side():
        for b in range(3):
            dacc[:, blk(b)] += lax.dot_general(Ar[slot[b]].T, up_act[blk(b)], TB, preferred_element_type=f32)

    def owned(recv, ss, rs, to):
        got(recv.at[pl.ds(1, 7)], ss.at[0], rs.at[0])
        picks = [wanted(rem(dp - k + 8, 8)) for k in range(8)]
        for a in range(4):
            v = None
            for k, (found, sel) in enumerate(picks):
                w = jnp.where((found == 1) & (sel == a), 1.0, 0.0).astype(f32)
                t = w * recv[k].astype(f32)
                v = t if v is None else v + t
            to[a] = v.astype(bf16)

    pl.semaphore_wait(bar, len(peers))
    def first(d, i):
        put(w_hbm.at[:, pl.ds(256 * i, 256)], Wp.at[wbase + i], w1S.at[d, i], w1R.at[d, i], (XP, XM)[d])

    def came(d, i):
        got(wsl(3 if d == 0 else 1, i, 1), w1S.at[d, i], w1R.at[d, i])

    first(0, 0); first(1, 2); first(0, 1); first(1, 3)
    loc[2].wait()
    gput(0, gsl(0, 0), ZP)
    gput(1, gsl(0, 0), ZM)
    gy(0)
    live = lives[dp]
    rows = lax.broadcasted_iota(jnp.int32, (384, 1), 0)
    own = [ids[3 * dp + b] // 4 for b in range(3)]
    slot = [rem(dp - own[b] + 8, 8) for b in range(3)]
    sels = [wanted(dps[k][0])[1] for k in range(8)]
    loc[0].wait()
    for k in range(8):
        (Br if k == 0 else Bs)[k] = b_ref[sels[k]]
    for k in range(1, 8):
        put(Bs.at[k], Br.at[k], bS.at[0], bR.at[0], dps[k], False)
    for cp in loc[5:]:
        cp.wait()
    wput(6, 0, 0, 4, SIB)
    first(0, 2); first(1, 0); first(0, 3); first(1, 1)
    loc[1].wait()
    masked[...] = jnp.where(rows < live, grad[...], jnp.zeros_like(grad))
    loc[3].wait()
    for k in range(8):
        (Ar if k == 0 else As)[k] = a_ref[sels[k]]
    dacc[...] = jnp.zeros_like(dacc)
    loc[4].wait()
    hid[...] = hid_t[...].T

    far = rem(y - x + 4, 4)
    r1 = rem(x + jnp.where(far == 2, 1, 0), 4)
    r2 = rem(x + jnp.where(far < 2, 1, 3), 4)
    r3 = rem(x + jnp.where(far < 2, 3, far - 2), 4)
    r4 = rem(x + 2, 4)

    wgot(6, 0, 0, 4, 1)
    both(0, 0)
    gz(1); gy(1); gy(2)
    both(0, 1)
    gz(2); gy(3); gy(4)
    both(0, 2)
    gz(3); gy(5); gy(6)
    came(0, 0); wput(4, 3, 0, 1, XP); came(0, 1); wput(5, 3, 1, 1, XP); wput(7, 3, 0, 2, SIB)
    came(1, 2); wput(13, 1, 2, 1, XM); came(1, 3); wput(14, 1, 3, 1, XM); wput(9, 1, 2, 2, SIB)
    for k in range(1, 8):
        put(As.at[k], Ar.at[k], aS.at[0], aR.at[0], dps[k], False)
    both(0, 3)
    up_scatter()
    wgot(7, 3, 0, 2, 1); wgot(9, 1, 2, 2, 1)
    both(1, 0)
    gz(4); gy(7)
    both(0, 4)
    fold_z(1)
    both(1, 1)
    gf(0); gf(1); gf(2)
    both(1, 2)
    fold_y(1)
    gf(3); gf(4)
    both(1, 3)
    gf(5); gf(6)
    came(0, 2); came(0, 3); wput(8, 3, 2, 2, SIB)
    came(1, 0); came(1, 1); wput(10, 1, 0, 2, SIB)
    up_terms()
    wgot(8, 3, 2, 2, 1); wgot(10, 1, 0, 2, 1)
    both(2, 0)
    gf(7)
    both(1, 4)
    backs(r1)
    both(2, 1)
    backs(r2)
    both(2, 2)
    for cp in sends:
        cp.wait_send()
    sends.clear()
    left(Bs.at[pl.ds(1, 7)], bS.at[0])
    left(part.at[1, pl.ds(0, 168)], p1S.at[1])
    left(fold_r.at[1, pl.ds(1, 3)], p2S.at[1])
    left(part.at[1, pl.ds(0, 168)], p3S.at[1])
    left(Gg.at[pl.ds(0, 16)], gyS.at[0])
    left(Zs.at[0], zS.at[0])
    left(Zs.at[1], zS.at[1])
    wgot(4, 2, 0, 1); wput(11, 2, 0, 1, SIB)
    wgot(13, 2, 2, 1); wput(12, 2, 2, 1, SIB)
    both(2, 3)
    wgot(5, 2, 1, 1); wput(15, 2, 1, 1, SIB)
    wgot(14, 2, 3, 1); wput(16, 2, 3, 1, SIB)
    both(2, 4)
    wgot(11, 2, 0, 1, 1); wgot(12, 2, 2, 1, 1); wgot(15, 2, 1, 1, 1); wgot(16, 2, 3, 1, 1)
    both(3, 0)
    pre(3, 1)
    gl()
    left(Gg.at[pl.ds(0, 8)], gfS.at[0])
    backs(r3)
    level(3, 1)
    pre(3, 2)
    down_scatter()
    level(3, 2)
    fold_z(0)
    pre(3, 3)
    backs(r4, 0, 2)
    level(3, 3)
    fold_y(0)
    left(As.at[pl.ds(1, 7)], aS.at[0])
    pre(3, 4)
    level(3, 4)
    down_terms()
    backs(r4, 2, 2)
    side()
    columns = lax.broadcasted_iota(jnp.int32, (1, 384), 1)
    dh[...] = jnp.where(columns < live, dacc[...], 0.0).astype(bf16)
    outs = [pltpu.make_async_copy(s, d, oS.at[i]) for i, (s, d) in enumerate(((out, out_h), (dh, dh_h), (dg, dg_h), (ug, ug_h)))]
    outs[1].start()
    owned(Tr, tS, tR, dg)
    outs[2].start()
    for b in range(3):
        acc[0, 0, blk(b)] = jnp.dot(down_act[blk(b)], Br[slot[b]], preferred_element_type=f32)
    for h in (0, 1):
        r = pl.ds(192 * h, 192)
        for j in range(3):
            got(Yr.at[j, h], yS.at[0, h], yR.at[j, h])
        t = acc[0, 0, r] + Sown[r]
        for j in range(3):
            t = t + Yr[j, h].astype(f32)
        out[r] = jnp.where(rows[192 * h:192 * h + 192] < live, t, 0.0).astype(bf16)

    outs[0].start()
    owned(Ur, uS, uR, ug)
    outs[3].start()
    for cp in sends:
        cp.wait_send()
    left(Us.at[pl.ds(1, 7)], uS.at[0])
    left(Ts.at[pl.ds(1, 7)], tS.at[0])
    left(part.at[0, pl.ds(0, 168)], p1S.at[0])
    left(fold_r.at[0, pl.ds(1, 3)], p2S.at[0])
    left(part.at[0, pl.ds(0, 168)], p3S.at[0])
    left(Zs.at[2], zS.at[2])
    left(Zs.at[3], zS.at[3])
    for r in range(4):
        @pl.when(y != row(r, z))
        def _():
            for h in (0, 1):
                ycopy(r, h).wait_send()
    for cp in outs:
        cp.wait()


def finish(*refs):
    ins, to, held, sems = refs[:4], refs[4:8], refs[8:12], refs[12]
    come = [pltpu.make_async_copy(ins[k], held[k], sems.at[0, k]) for k in range(4)]
    go = [pltpu.make_async_copy(held[k], to[k], sems.at[1, k]) for k in range(4)]
    for cp in come:
        cp.start()
    for k in range(4):
        come[k].wait()
        go[k].start()
    for cp in go:
        cp.wait()


def shards(hidden, down_weight, adapter_down, adapter_up, output_grad, adapter_per_block, live_rows):
    V = pl.BlockSpec(memory_space=pltpu.VMEM)
    S = pl.BlockSpec(memory_space=pltpu.SMEM)
    A = pl.BlockSpec(memory_space=pl.ANY)
    D = pltpu.SemaphoreType.DMA
    M = pltpu.VMEM
    out, dh_t, dg_t, ug = pl.pallas_call(
        kernel,
        out_shape=(
            jax.ShapeDtypeStruct((384, 256), bf16), jax.ShapeDtypeStruct((832, 384), bf16),
            jax.ShapeDtypeStruct((4, 64, 832), bf16), jax.ShapeDtypeStruct((4, 64, 256), bf16)),
        in_specs=[S, S, A, A, A, A, A],
        out_specs=(A, A, A, A),
        scratch_shapes=[
            M((384, 256), bf16), M((832, 384), bf16), M((4, 64, 832), bf16), M((4, 64, 256), bf16), D((4,)),
            M((832, 384), bf16), M((384, 832), bf16), M((384, 256), bf16), M((384, 256), bf16),
            M((4, 64, 832), bf16), M((4, 64, 256), bf16),
            M((32, 832, 256), bf16),
            M((32, 384, 256), bf16),
            M((4, 7, 2, 192, 256), bf16),
            M((4, 7, 2, 192, 256), bf16),
            M((4, 2, 192, 256), bf16),
            M((3, 2, 192, 256), bf16),
            M((384, 256), f32),
            M((2, 2, 384, 256), f32),
            M((832, 384), f32),
            M((8, 64, 832), bf16), M((8, 64, 832), bf16), M((8, 64, 256), bf16), M((8, 64, 256), bf16),
            M((8, 64, 832), bf16), M((8, 64, 832), bf16), M((8, 64, 256), bf16), M((8, 64, 256), bf16),
            M((3, 64, 832), bf16), M((3, 64, 256), bf16),
            M((2, 192, 128), f32), M((2, 8, 24, 128), f32), M((2, 24, 128), f32), M((2, 4, 24, 128), f32), M((2, 192, 128), f32),
            M((384, 64), bf16), M((384, 64), bf16),
            D((9,)), D((17,)), D((17,)), D((2, 4)), D((2, 4)), D((8,)), D((8,)), D((1,)), D((8, 2)), D((1,)), D((1,)),
            D((4,)), D((4, 7, 2)), D((4, 2)), D((3, 2)),
            D((1,)), D((1,)), D((1,)), D((1,)), D((1,)), D((1,)), D((1,)), D((1,)),
            D((2,)), D((2,)), D((2,)), D((2,)), D((2,)), D((2,)),
        ],
        name="layer",
        cost_estimate=pl.CostEstimate(flops=2 * 2 * 384 * 832 * 8192, bytes_accessed=6 * 2 ** 20, transcendentals=0),
        compiler_params=pltpu.CompilerParams(collective_id=0, has_side_effects=True, vmem_limit_bytes=58 * 2 ** 20),
    )(adapter_per_block, live_rows, hidden.T, down_weight, jnp.swapaxes(adapter_down, 1, 2), adapter_up, output_grad)
    parts = (out, dh_t, dg_t, ug)
    out, dh_t, dg_t, ug = pl.pallas_call(
        finish,
        out_shape=tuple(jax.ShapeDtypeStruct(v.shape, v.dtype) for v in parts),
        in_specs=[A] * 4, out_specs=(A,) * 4,
        scratch_shapes=[M(v.shape, v.dtype) for v in parts] + [D((2, 4))], name="finish",
        cost_estimate=pl.CostEstimate(flops=0, bytes_accessed=4 * 2 ** 20, transcendentals=0),
    )(*parts)
    return out, dh_t.T, jnp.swapaxes(dg_t, 1, 2), ug


def solution(mesh):
    return jax.shard_map(
        shards,
        mesh=mesh,
        in_specs=(P("dp", "mp"), P("mp", "dp"), P("dp", "mp", None), P("dp", None, "mp"), P("dp", "mp"), P(), P()),
        out_specs=(P("dp", "mp"), P("dp", "mp"), P("dp", "mp", None), P("dp", None, "mp")),
        check_vma=False,
    )
```
